32 devices in a mesh: seq: 8 (over z, y), head: 4 (over x, core).
Axes of the slice: x: 2, y: 2, z: 4, core: 2. Of those that a mesh axis runs over, the one named last changes fastest.
Arguments:
- tokens: bfloat16 [8192, 4096], P('seq'), may hold values from -50 to 50
- norm_gain: float32 [4096], replicated, may hold values from 0.1 to 1.9
- wq: bfloat16 [4096, 4096], P('seq', 'head'), may hold values from -2.34375 to 2.34375
- wk: bfloat16 [4096, 1024], P('seq', 'head'), may hold values from -0.09375 to 0.09375
- wv: bfloat16 [4096, 1024], P('seq', 'head'), may hold values from -0.09375 to 0.09375
- wo: bfloat16 [4096, 4096], P('head', 'seq'), may hold values from -0.125 to 0.125
- gate_bias: float32 [32], P('head'), may hold values from -3 to 3
- mem_init: float32 [8, 128, 128], P('head'), may hold values from -32768 to 32768
- norm_init: float32 [8, 128], P('head'), may hold values from 512 to 2048
Outputs:
- attended: bfloat16 [8192, 4096], P('seq', 'head')
The draws below stay inside these ranges and needn't reach their ends.
All inputs are finite; a program needn't handle non-finite values.
Results may differ from the reference program's by a relative error of at most 0.018.
Values may be sent and summed in bfloat16 or wider, within the bound.
A program may use at most 128 MiB of HBM per device.

```python
import math
import jax
import jax.numpy as jnp
from jax import lax

D = 4096
H = 32
KVH = 8
HD = 128
SEG = 512
TOK_DEV = 1024
TOKENS = 8192
N_HEAD = 4


def shared_keys(key):
    base_draw = jax.random.normal(jax.random.fold_in(key, 11), (D, KVH * HD), jnp.float32)
    return jnp.clip(base_draw, -6.0, 6.0) / math.sqrt(D)


def draw_wk(key, part):
    return shared_keys(key).astype(jnp.bfloat16)


def draw_wq(key, part):
    noise = jax.random.normal(jax.random.fold_in(key, 12), (D, H * HD), jnp.float32)
    noise = jnp.clip(noise, -6.0, 6.0) / math.sqrt(D)
    return noise.astype(jnp.bfloat16)


def draw_tokens(key, part):
    first_key = jax.random.fold_in(key, 21)
    second_key = jax.random.fold_in(key, 22)
    offsets = jnp.clip(jax.random.normal(second_key, (TOKENS // SEG, D), jnp.float32), -3.0, 3.0)
    noise = jnp.clip(jax.random.normal(first_key, (TOKENS, D), jnp.float32), -5.0, 5.0)
    rows = noise + jnp.repeat(offsets, SEG, axis=0)
    rows = jnp.clip(rows, -50.0, 50.0)
    return rows.astype(jnp.bfloat16)


def raised(array, own_key, source, target, shards_of, factor):
    def block_of(dim):
        return (jnp.arange(array.shape[dim]) // (array.shape[dim] // shards_of)).reshape((-1,) + (1,) * (array.ndim - 1 - dim))

    near = jax.random.permutation(own_key, shards_of)[block_of(target)]
    other_side = (block_of(target) + shards_of // 2) % shards_of
    return jnp.where((block_of(source) == near) | (block_of(source) == other_side), factor * array, array)


def block_levels(key, extent, cuts, smallest, top_value):
    loudness, own = 1.0, jax.random.fold_in(key, 6)
    for position, blocks in cuts:
        heights = jnp.exp(jax.random.uniform(jax.random.fold_in(own, position), (blocks,), jnp.float32, smallest / len(cuts), top_value / len(cuts)))
        loudness = loudness * jnp.repeat(heights, extent[position] // blocks).reshape([-1 if axis == position else 1 for axis in range(len(extent))])
    return loudness


def normal_values(key, extent, spread, limit, split=(), dtype=jnp.bfloat16):
    level = block_levels(key, extent, split, -0.22, 0.18) if split else 1.0
    drawn = jax.random.normal(key, extent, jnp.float32) * spread * level
    return jnp.minimum(jnp.maximum(drawn, -limit), limit).astype(dtype)


def heavy_noise(stream_key, extent, width, most, shards, heavy, dtype=jnp.bfloat16):
    result = width * jax.random.normal(stream_key, extent, jnp.float32)
    if shards:
        result = result * block_levels(stream_key, extent, shards, -0.22, 0.18)
    return jnp.clip(raised(result, jax.random.fold_in(stream_key, 3), *heavy), -most, most).astype(dtype)


def setup_inputs(seed: int = 0) -> dict:
    splits = jax.random.split(jax.random.key(seed), 10)
    tokens = draw_tokens(jax.random.fold_in(splits[9], 71), 0)
    norm_gain = jnp.clip(1.0 + 0.18 * jax.random.normal(splits[1], (D,), jnp.float32), 0.1, 1.9)
    wq = draw_wq(jax.random.fold_in(splits[9], 71), 0)
    wk = draw_wk(jax.random.fold_in(splits[9], 71), 0)
    wv = normal_values(splits[4], (D, KVH * HD), D ** -0.5, 0.09375, ((0, 8), (1, 4)))
    wo = heavy_noise(splits[5], (H * HD, D), (H * HD) ** -0.5, 0.125, ((0, 4), (1, 8)), (0, 1, 8, 2.0))
    gate_bias = jnp.clip(jax.random.uniform(splits[6], (H,), jnp.float32, -3.0, 3.0) * block_levels(splits[6], (H,), ((0, 4),), -0.4, 0.0), -3.0, 3.0)
    mem_init = normal_values(splits[7], (KVH, HD, HD), (6 * TOK_DEV), 32768.0, ((0, 4),), jnp.float32)
    norm_init = jnp.clip(512.0 + 1536.0 * jax.random.uniform(splits[8], (KVH, HD), jnp.float32) ** block_levels(splits[8], (KVH, HD), ((0, 4),), -0.2, 0.2), 512.0, 2048.0)
    return dict(tokens=tokens, norm_gain=norm_gain, wq=wq, wk=wk, wv=wv, wo=wo, gate_bias=gate_bias, mem_init=mem_init, norm_init=norm_init)


def feature_map(values_in):
    return jnp.where(values_in > 0, values_in + 1.0, jnp.exp(jnp.minimum(values_in, 0.0)))

def reference(tokens, norm_gain, wq, wk, wv, wo, gate_bias, mem_init, norm_init):
    highest = lax.Precision.HIGHEST
    widened = tokens.astype(jnp.float32)
    normed = (widened * lax.rsqrt(lax.optimization_barrier(jnp.mean(widened * widened, axis=-1, keepdims=True)) + 1e-05) * norm_gain).astype(jnp.bfloat16)
    queries = jnp.dot(normed, wq, preferred_element_type=jnp.float32).astype(jnp.bfloat16)
    keys_all = jnp.dot(normed, wk, preferred_element_type=jnp.float32).astype(jnp.bfloat16)
    values_all = jnp.dot(normed, wv, preferred_element_type=jnp.float32).astype(jnp.bfloat16)
    group = H // KVH
    segments = TOKENS // SEG
    query_seg = queries.reshape(segments, SEG, KVH, group, HD)
    key_seg = keys_all.reshape(segments, SEG, KVH, HD)
    value_seg = values_all.reshape(segments, SEG, KVH, HD)
    key_feats = feature_map(key_seg.astype(jnp.float32))
    delta_mem = jnp.einsum('nski,nskj->nkij', key_feats, value_seg.astype(jnp.float32), precision=highest)
    delta_norm = lax.optimization_barrier(jnp.sum(key_feats, axis=1))
    zero_mem = jnp.zeros((1, KVH, HD, HD), jnp.float32)
    zero_norm = jnp.zeros((1, KVH, HD), jnp.float32)
    mem_before = mem_init[None] + jnp.concatenate([zero_mem, jnp.cumsum(delta_mem, axis=0)[:-1]], axis=0)
    norm_before = norm_init[None] + jnp.concatenate([zero_norm, jnp.cumsum(delta_norm, axis=0)[:-1]], axis=0)
    gate_mix = jax.nn.sigmoid(gate_bias).reshape(KVH, group)
    score_scale = 1.0 / math.sqrt(HD)
    causal = lax.broadcasted_iota(jnp.int32, (SEG, SEG), 0) >= lax.broadcasted_iota(jnp.int32, (SEG, SEG), 1)

    def one_segment(operands):
        query_blk, key_blk, value_blk, memory, normer = operands
        query_feats = feature_map(query_blk.astype(jnp.float32))
        numer = jnp.einsum('skgi,kij->skgj', query_feats, memory, precision=highest)
        denom = jnp.einsum('skgi,ki->skg', query_feats, normer, precision=highest)
        retrieved = numer / denom[..., None]
        scores = jnp.einsum('qkgd,skd->kgqs', query_blk.astype(jnp.float32), key_blk.astype(jnp.float32), precision=highest) * score_scale
        scores = jnp.where(causal, scores, -1e+30)
        peak = lax.optimization_barrier(jnp.max(scores, axis=-1, keepdims=True))
        expd = jnp.exp(scores - peak)
        probs = (expd / lax.optimization_barrier(jnp.sum(expd, axis=-1, keepdims=True))).astype(jnp.bfloat16)
        local = jnp.einsum('kgqs,skd->qkgd', probs.astype(jnp.float32), value_blk.astype(jnp.float32), precision=highest)
        mixed = gate_mix[None, :, :, None] * retrieved + (1.0 - gate_mix)[None, :, :, None] * local
        return mixed.astype(jnp.bfloat16)
    mixed_all = lax.map(one_segment, (query_seg, key_seg, value_seg, mem_before, norm_before))
    mixed_all = mixed_all.reshape(TOKENS, H * HD)
    width_group = H * HD // N_HEAD
    summed = jnp.zeros((TOKENS, D), jnp.float32)
    for block in range(N_HEAD):
        partial_out = jnp.dot(mixed_all[:, block * width_group:(block + 1) * width_group], wo[block * width_group:(block + 1) * width_group], preferred_element_type=jnp.float32)
        rounded = lax.optimization_barrier(partial_out.astype(jnp.bfloat16))
        summed = summed + rounded.astype(jnp.float32)
    return summed.astype(jnp.bfloat16)
```

```python
import functools
import math

import jax
import jax.numpy as jnp
from jax import lax
from jax.experimental import pallas as pl
from jax.experimental.pallas import tpu as pltpu
from jax.sharding import PartitionSpec as P

HD = 128
SEG = 512
NORM_ROWS = 16
MEM_ROWS = HD + NORM_ROWS
MESH = pl.DeviceIdType.MESH
KV, Q, WO, MEM = range(4)


def feature_map(values_in):
    return jnp.where(values_in > 0, values_in + 1.0, jnp.exp(jnp.minimum(values_in, 0.0)))


def layer_kernel(
    n,
    heads_axis,
    tokens,
    gain,
    wq,
    wk,
    wv,
    wo,
    gates,
    mem_init,
    norm_init,
    out,
    normed,
    kv_full,
    q_full,
    wo_full,
    mem_full,
    acc_kv,
    acc_q,
    keys,
    vals,
    queries,
    deltas,
    delta_norms,
    memory,
    mixed,
    got,
    xgot,
    ring_send,
    ring_recv,
    give_send,
    give_recv,
    x_send,
    x_recv,
    load_sem,
):
    me = lax.axis_index("seq")
    head = lax.axis_index("head")
    hops = n // 2
    per_head = n // heads_axis
    rows_in = wq.shape[0]
    token_count = tokens.shape[0]
    kv_width = wk.shape[1]
    q_heads = wq.shape[1] // HD
    kv_heads = kv_width // HD
    group = q_heads // kv_heads
    segments = token_count // SEG
    width = tokens.shape[1]
    block = wo.shape[1]
    tile = 256

    odd = lax.rem(me, 2)
    pos = (1 - odd) * lax.div(me, 2) + odd * (n - 1 - lax.div(me, 2))

    def seq_of(place):
        place = lax.rem(place + n, n)
        far = lax.div(place, hops)
        return (1 - far) * 2 * place + far * (2 * (n - place) - 1)

    sides = (seq_of(pos + 1), seq_of(pos - 1))
    core = lax.rem(head, 2)
    partner = head + 1 - 2 * core
    across = lax.rem(head + heads_axis // 2, heads_axis)

    loads = [
        pltpu.make_async_copy(wk, kv_full.at[me, :, pl.ds(0, kv_width)], load_sem.at[0]),
        pltpu.make_async_copy(wv, kv_full.at[me, :, pl.ds(kv_width, kv_width)], load_sem.at[1]),
        pltpu.make_async_copy(wq, q_full.at[me], load_sem.at[2]),
        pltpu.make_async_copy(wo, wo_full.at[me], load_sem.at[3]),
    ]
    for i in range(n):
        loads.append(
            pltpu.make_async_copy(
                tokens.at[:, pl.ds(i * rows_in, rows_in)], normed.at[i], load_sem.at[4 + i]
            )
        )
    for load in loads:
        load.start()

    barrier = pltpu.get_barrier_semaphore()
    for side in sides:
        pl.semaphore_signal(barrier, inc=1, device_id=(side, head), device_id_type=MESH)
    for other in (partner, across):
        pl.semaphore_signal(barrier, inc=1, device_id=(me, other), device_id_type=MESH)
    pl.semaphore_wait(barrier, 4)

    fulls = (kv_full, q_full, wo_full, mem_full)

    def ring(kind, way, hop, part):
        owner = seq_of(pos - hop + 1) if way == 0 else seq_of(pos + hop - 1)
        half = fulls[kind].shape[1] // 2
        view = fulls[kind].at[owner, pl.ds(part * half, half)]
        return pltpu.make_async_remote_copy(
            src_ref=view,
            dst_ref=view,
            send_sem=ring_send.at[kind, way, hop - 1, part],
            recv_sem=ring_recv.at[kind, way, hop - 1, part],
            device_id=(sides[way], head),
            device_id_type=MESH,
        )

    def arrival(kind, way, hop, part):
        owner = seq_of(pos - hop) if way == 0 else seq_of(pos + hop)
        half = fulls[kind].shape[1] // 2
        view = fulls[kind].at[owner, pl.ds(part * half, half)]
        return pltpu.make_async_remote_copy(
            src_ref=view,
            dst_ref=view,
            send_sem=ring_send.at[kind, way, hop - 1, part],
            recv_sem=ring_recv.at[kind, way, hop - 1, part],
            device_id=(sides[way], head),
            device_id_type=MESH,
        )

    def send_first(kind):
        for part in range(2):
            for way in range(2):
                ring(kind, way, 1, part).start()

    def forward(kind, hop):
        for step in range(2):
            for way in range(2):
                part = step if way == 0 else 1 - step
                arrival(kind, way, hop, part).wait_recv()
                if step == 0:
                    ring(kind, way, hop + 1, part).start()
                else:

                    @pl.when(hop + 1 < hops)
                    def _():
                        ring(kind, way, hop + 1, part).start()

    def take_last(kind):
        for way in range(2):
            arrival(kind, way, hops, way).wait_recv()

    loads[0].wait()
    loads[1].wait()
    send_first(KV)
    loads[2].wait()
    send_first(Q)
    loads[3].wait()
    for load in loads[4:]:
        load.wait()

    def norm_rows(i, carry):
        rows = pl.ds(pl.multiple_of(i * 64, 64), 64)
        total = jnp.zeros((64, 1), jnp.float32)
        for b in range(n):
            x = normed[b, rows, :].astype(jnp.float32)
            total = total + jnp.sum(x * x, axis=-1, keepdims=True)
        scale = lax.rsqrt(total * (1.0 / width) + 1e-05)
        for b in range(n):
            x = normed[b, rows, :].astype(jnp.float32)
            normed[b, rows, :] = (x * scale * gain[b]).astype(jnp.bfloat16)
        return carry

    lax.fori_loop(0, token_count // 64, norm_rows, 0)

    def project(acc, full, owner, first=False):
        def body(i, carry):
            rows = pl.ds(pl.multiple_of(i * tile, tile), tile)
            product = jnp.dot(
                normed[owner, rows, :], full[owner], preferred_element_type=jnp.float32
            )
            if first:
                acc[rows, :] = product
            else:
                acc[rows, :] += product
            return carry

        lax.fori_loop(0, token_count // tile, body, 0)

    def project_hop(acc, full, hop):
        def body(side, carry):
            project(acc, full, seq_of(pos - hop + 2 * hop * side))
            return carry

        lax.fori_loop(0, 2, body, 0)

    project(acc_kv, kv_full, me, True)

    def kv_step(hop, carry):
        forward(KV, hop)
        project_hop(acc_kv, kv_full, hop)
        return carry

    lax.fori_loop(1, hops, kv_step, 0)
    take_last(KV)
    forward(Q, 1)
    project(acc_kv, kv_full, seq_of(pos + hops))

    for j in range(kv_heads):
        for s in range(segments):
            rows = slice(s * SEG, (s + 1) * SEG)
            key = acc_kv[rows, j * HD : (j + 1) * HD].astype(jnp.bfloat16)
            value = acc_kv[rows, kv_width + j * HD : kv_width + (j + 1) * HD].astype(jnp.bfloat16)
            keys[j, rows, :] = key
            vals[j, rows, :] = value
            feats = feature_map(key.astype(jnp.float32))
            deltas[s, j] = jnp.dot(
                feats.T.astype(jnp.bfloat16), value, preferred_element_type=jnp.float32
            )
            delta_norms[s, j] = jnp.broadcast_to(jnp.sum(feats, axis=0, keepdims=True), (8, HD))
        own = deltas[0, j]
        own_norm = delta_norms[0, j]
        for s in range(1, segments):
            own = own + deltas[s, j]
            own_norm = own_norm + delta_norms[s, j]
        mem_full[me, j * MEM_ROWS : j * MEM_ROWS + HD, :] = own.astype(jnp.bfloat16)
        mem_full[me, j * MEM_ROWS + HD : (j + 1) * MEM_ROWS, :] = jnp.concatenate(
            [own_norm, own_norm], axis=0
        ).astype(jnp.bfloat16)
    send_first(MEM)

    project(acc_q, q_full, me, True)
    project_hop(acc_q, q_full, 1)

    def q_step(hop, carry):
        forward(Q, hop)
        forward(MEM, hop - 1)
        project_hop(acc_q, q_full, hop)
        return carry

    lax.fori_loop(2, hops, q_step, 0)
    send_first(WO)
    forward(MEM, hops - 1)
    take_last(Q)
    project(acc_q, q_full, seq_of(pos + hops))
    for h in range(q_heads):
        queries[h] = acc_q[:, h * HD : (h + 1) * HD].astype(jnp.bfloat16)

    score_scale = 1.0 / math.sqrt(HD)
    half_seg = SEG // 2

    def attend(h, carry):
        j = lax.div(h, group)
        columns = pl.ds(pl.multiple_of(h * HD, HD), HD)
        for s in range(segments):
            for t in range(2):
                start = s * SEG + t * half_seg
                seen = (t + 1) * half_seg
                scores = (
                    lax.dot_general(
                        queries[h, start : start + half_seg, :],
                        keys[j, s * SEG : s * SEG + seen, :],
                        (((1,), (1,)), ((), ())),
                        preferred_element_type=jnp.float32,
                    )
                    * score_scale
                )
                at_row = lax.broadcasted_iota(jnp.int32, (half_seg, seen), 0) + t * half_seg
                at_col = lax.broadcasted_iota(jnp.int32, (half_seg, seen), 1)
                scores = jnp.where(at_row >= at_col, scores, -1e30)
                expd = jnp.exp(scores - jnp.max(scores, axis=-1, keepdims=True))
                total = jnp.sum(expd, axis=-1, keepdims=True)
                summed = jnp.dot(
                    expd.astype(jnp.bfloat16),
                    vals[j, s * SEG : s * SEG + seen, :],
                    preferred_element_type=jnp.float32,
                )
                acc_q[start : start + half_seg, columns] = summed / total
        return carry

    lax.fori_loop(0, q_heads // 2, attend, 0)
    forward(WO, 1)
    lax.fori_loop(q_heads // 2, q_heads, attend, 0)

    take_last(MEM)
    for j in range(kv_heads):

        def add_earlier(s, carry):
            mem, norm = carry
            earlier = mem_full[s, j * MEM_ROWS : (j + 1) * MEM_ROWS, :].astype(jnp.float32)
            return mem + earlier[:HD], norm + earlier[HD : HD + 8]

        mem, norm = lax.fori_loop(
            0,
            me,
            add_earlier,
            (mem_init[j], jnp.broadcast_to(norm_init[j], (8, HD))),
        )
        for s in range(segments):
            memory[s, j, :, :HD] = mem.astype(jnp.bfloat16)
            memory[s, j, :, HD:] = jnp.broadcast_to(norm[:1], (HD, HD)).T.astype(jnp.bfloat16)
            if s + 1 < segments:
                mem = mem + deltas[s, j]
                norm = norm + delta_norms[s, j]

    def retrieve(h, carry):
        j = lax.div(h, group)
        columns = pl.ds(pl.multiple_of(h * HD, HD), HD)
        gate = gates[h]
        for s in range(segments):
            rows = slice(s * SEG, (s + 1) * SEG)
            feats = feature_map(queries[h, rows, :].astype(jnp.float32)).astype(jnp.bfloat16)
            both = jnp.dot(feats, memory[s, j], preferred_element_type=jnp.float32)
            retrieved = both[:, :HD] / both[:, HD:]
            mixed[rows, columns] = (
                gate * retrieved + (1.0 - gate) * acc_q[rows, columns]
            ).astype(jnp.bfloat16)
        return carry

    lax.fori_loop(0, q_heads, retrieve, 0)

    def place_of(c):
        target = lax.div(c, per_head)
        slot = lax.div(target, 2) * per_head + lax.rem(c, per_head)
        return target, slot

    def give(c):
        target, slot = place_of(c)
        return pltpu.make_async_remote_copy(
            src_ref=normed.at[c],
            dst_ref=got.at[slot],
            send_sem=give_send.at[slot],
            recv_sem=give_recv.at[slot],
            device_id=(me, partner),
            device_id_type=MESH,
        )

    def cross(c):
        return pltpu.make_async_remote_copy(
            src_ref=normed.at[c],
            dst_ref=xgot.at[lax.rem(c, per_head)],
            send_sem=x_send.at[lax.rem(c, per_head)],
            recv_sem=x_recv.at[lax.rem(c, per_head)],
            device_id=(me, across),
            device_id_type=MESH,
        )

    def emit(c):
        def body(i, carry):
            rows = pl.ds(pl.multiple_of(i * tile, tile), tile)
            normed[c, rows, :] = jnp.dot(
                mixed[rows, :], wo_full[c], preferred_element_type=jnp.float32
            ).astype(jnp.bfloat16)
            return carry

        lax.fori_loop(0, token_count // tile, body, 0)
        target, slot = place_of(c)

        @pl.when(lax.rem(target, 2) != core)
        def _():
            give(c).start()

    def finish(c):
        target, slot = place_of(c)

        @pl.when(lax.rem(target, 2) == core)
        def _():
            give(c).wait_recv()

            def body(i, carry):
                rows = pl.ds(pl.multiple_of(i * tile, tile), tile)
                normed[c, rows, :] = (
                    normed[c, rows, :].astype(jnp.float32) + got[slot, rows, :].astype(jnp.float32)
                ).astype(jnp.bfloat16)
                return carry

            @pl.when(target != head)
            def _():
                lax.fori_loop(0, token_count // tile, body, 0)
                cross(c).start()

    emit(me)
    finish(me)

    def out_step(hop, carry):
        def emit_side(side, inner):
            emit(seq_of(pos - hop + 2 * hop * side))
            return inner

        def finish_side(side, inner):
            finish(seq_of(pos - hop + 2 * hop * side))
            return inner

        lax.fori_loop(0, 2, emit_side, 0)
        lax.fori_loop(0, 2, finish_side, 0)

        @pl.when(hop + 1 < hops)
        def _():
            forward(WO, hop + 1)

        return carry

    lax.fori_loop(1, hops, out_step, 0)
    take_last(WO)
    emit(seq_of(pos + hops))
    finish(seq_of(pos + hops))

    for o in range(per_head):
        c = head * per_head + o
        cross(c).wait_recv()
        slot = lax.div(head, 2) * per_head + o

        def body(i, carry):
            rows = pl.ds(pl.multiple_of(i * tile, tile), tile)
            out[rows, o * block : (o + 1) * block] = (
                normed[c, rows, :].astype(jnp.float32)
                + got[slot, rows, :].astype(jnp.float32)
                + xgot[o, rows, :].astype(jnp.float32)
            ).astype(jnp.bfloat16)
            return carry

        lax.fori_loop(0, token_count // tile, body, 0)

    for kind in range(4):

        def drain(hop, carry):
            for way in range(2):
                for part in range(2):
                    ring(kind, way, hop, part).wait_send()
            return carry

        lax.fori_loop(1, hops, drain, 0)
        for way in range(2):
            ring(kind, way, hops, way).wait_send()

    def drain_out(c, carry):
        target, slot = place_of(c)

        @pl.when(lax.rem(target, 2) != core)
        def _():
            give(c).wait_send()

        @pl.when((lax.rem(target, 2) == core) & (target != head))
        def _():
            cross(c).wait_send()

        return carry

    lax.fori_loop(0, n, drain_out, 0)


def per_device(n, heads_axis, tokens, norm_gain, wq, wk, wv, wo, gate_bias, mem_init, norm_init):
    token_count, width = tokens.shape
    rows_in = wq.shape[0]
    q_width = wq.shape[1]
    kv_width = wk.shape[1]
    q_heads = q_width // HD
    kv_heads = kv_width // HD
    block = wo.shape[1]
    segments = token_count // SEG
    hops = n // 2
    per_head = n // heads_axis
    gates = jnp.broadcast_to(jax.nn.sigmoid(gate_bias)[:, None, None], (q_heads, 1, HD))
    gain = norm_gain.reshape(n, 1, rows_in)
    anywhere = pl.BlockSpec(memory_space=pl.ANY)
    near = pl.BlockSpec(memory_space=pltpu.VMEM)
    bf16, f32 = jnp.bfloat16, jnp.float32
    flops = 2 * token_count * (width * (q_width + 2 * kv_width) + q_width * width)
    return pl.pallas_call(
        functools.partial(layer_kernel, n, heads_axis),
        out_shape=jax.ShapeDtypeStruct((token_count, per_head * block), bf16),
        in_specs=[anywhere, near, anywhere, anywhere, anywhere, anywhere, near, near, near],
        out_specs=near,
        scratch_shapes=[
            pltpu.VMEM((n, token_count, rows_in), bf16),
            pltpu.VMEM((n, rows_in, 2 * kv_width), bf16),
            pltpu.VMEM((n, rows_in, q_width), bf16),
            pltpu.VMEM((n, q_width, block), bf16),
            pltpu.VMEM((n, kv_heads * MEM_ROWS, HD), bf16),
            pltpu.VMEM((token_count, 2 * kv_width), f32),
            pltpu.VMEM((token_count, q_width), f32),
            pltpu.VMEM((kv_heads, token_count, HD), bf16),
            pltpu.VMEM((kv_heads, token_count, HD), bf16),
            pltpu.VMEM((q_heads, token_count, HD), bf16),
            pltpu.VMEM((segments, kv_heads, HD, HD), f32),
            pltpu.VMEM((segments, kv_heads, 8, HD), f32),
            pltpu.VMEM((segments, kv_heads, HD, 2 * HD), bf16),
            pltpu.VMEM((token_count, q_width), bf16),
            pltpu.VMEM((n // 2, token_count, block), bf16),
            pltpu.VMEM((per_head, token_count, block), bf16),
            pltpu.SemaphoreType.DMA((4, 2, hops, 2)),
            pltpu.SemaphoreType.DMA((4, 2, hops, 2)),
            pltpu.SemaphoreType.DMA((n // 2,)),
            pltpu.SemaphoreType.DMA((n // 2,)),
            pltpu.SemaphoreType.DMA((per_head,)),
            pltpu.SemaphoreType.DMA((per_head,)),
            pltpu.SemaphoreType.DMA((4 + n,)),
        ],
        compiler_params=pltpu.CompilerParams(
            collective_id=0, has_side_effects=True, vmem_limit_bytes=60 * 1024 * 1024
        ),
        cost_estimate=pl.CostEstimate(
            flops=flops, bytes_accessed=2 * token_count * width, transcendentals=0
        ),
    )(tokens, gain, wq, wk, wv, wo, gates, mem_init, norm_init.reshape(kv_heads, 1, HD))


def solution(mesh):
    placed = (
        P("seq", None),
        P(),
        P("seq", "head"),
        P("seq", "head"),
        P("seq", "head"),
        P("head", "seq"),
        P("head"),
        P("head", None, None),
        P("head", None),
    )
    return jax.shard_map(
        functools.partial(per_device, mesh.shape["seq"], mesh.shape["head"]),
        mesh=mesh,
        in_specs=placed,
        out_specs=P("seq", "head"),
        check_vma=False,
    )
```

```python
import functools
import math

import jax
import jax.numpy as jnp
from jax import lax
from jax.experimental import pallas as pl
from jax.experimental.pallas import tpu as pltpu
from jax.sharding import PartitionSpec as P

HD = 128
SEG = 512
NORM_ROWS = 16
MEM_ROWS = HD + NORM_ROWS
MESH = pl.DeviceIdType.MESH
LOG2E = math.log2(math.e)


def feature_map(values_in):
    return jnp.where(values_in > 0, values_in + 1.0, jnp.exp(jnp.minimum(values_in, 0.0)))


def layer_kernel(
    n,
    heads_axis,
    wo_parts,
    tokens,
    gain,
    wq,
    wk,
    wv,
    wo,
    gates,
    mem_init,
    norm_init,
    out,
    normed,
    kv_full,
    q_full,
    wo_full,
    mem_full,
    acc_kv,
    acc_q,
    keys,
    vals,
    queries,
    deltas,
    delta_norms,
    memory,
    mixed,
    got,
    xgot,
    ring_send,
    ring_recv,
    give_send,
    give_recv,
    x_send,
    x_recv,
    load_sem,
):
    me = lax.axis_index("seq")
    head = lax.axis_index("head")
    hops = n // 2
    per_head = n // heads_axis
    rows_in = wq.shape[0]
    token_count = tokens.shape[0]
    kv_width = wk.shape[1]
    q_width = wq.shape[1]
    q_part = q_width // 2
    q_heads = q_width // HD
    kv_heads = kv_width // HD
    group = q_heads // kv_heads
    segments = token_count // SEG
    width = tokens.shape[1]
    block = wo.shape[1]
    sub = block // wo_parts
    tile = 256
    kv_kind, q_kinds = 0, (1, 2)
    wo_kinds = tuple(range(3, 3 + wo_parts))
    mem_kind = 3 + wo_parts

    odd = lax.rem(me, 2)
    pos = (1 - odd) * lax.div(me, 2) + odd * (n - 1 - lax.div(me, 2))

    def seq_of(place):
        place = lax.rem(place + n, n)
        far = lax.div(place, hops)
        return (1 - far) * 2 * place + far * (2 * (n - place) - 1)

    sides = (seq_of(pos + 1), seq_of(pos - 1))
    core = lax.rem(head, 2)
    partner = head + 1 - 2 * core
    across = lax.rem(head + heads_axis // 2, heads_axis)

    loads = [
        pltpu.make_async_copy(wk, kv_full.at[me, :, pl.ds(0, kv_width)], load_sem.at[0]),
        pltpu.make_async_copy(wv, kv_full.at[me, :, pl.ds(kv_width, kv_width)], load_sem.at[1]),
    ]
    for part in range(2):
        loads.append(
            pltpu.make_async_copy(
                wq.at[:, pl.ds(part * q_part, q_part)], q_full.at[part, me], load_sem.at[2 + part]
            )
        )
    for part in range(wo_parts):
        loads.append(
            pltpu.make_async_copy(
                wo.at[:, pl.ds(part * sub, sub)], wo_full.at[part, me], load_sem.at[4 + part]
            )
        )
    weight_loads = len(loads)
    for i in range(n):
        loads.append(
            pltpu.make_async_copy(
                tokens.at[:, pl.ds(i * rows_in, rows_in)], normed.at[i], load_sem.at[weight_loads + i]
            )
        )
    for load in loads:
        load.start()

    barrier = pltpu.get_barrier_semaphore()
    for side in sides:
        pl.semaphore_signal(barrier, inc=1, device_id=(side, head), device_id_type=MESH)
    for other in (partner, across):
        pl.semaphore_signal(barrier, inc=1, device_id=(me, other), device_id_type=MESH)
    pl.semaphore_wait(barrier, 4)

    fulls = [kv_full, q_full.at[0], q_full.at[1]]
    fulls += [wo_full.at[part] for part in range(wo_parts)]
    fulls.append(mem_full)

    def ring(kind, way, hop, part):
        owner = seq_of(pos - hop + 1) if way == 0 else seq_of(pos + hop - 1)
        half = fulls[kind].shape[1] // 2
        view = fulls[kind].at[owner, pl.ds(part * half, half)]
        return pltpu.make_async_remote_copy(
            src_ref=view,
            dst_ref=view,
            send_sem=ring_send.at[kind, way, hop - 1, part],
            recv_sem=ring_recv.at[kind, way, hop - 1, part],
            device_id=(sides[way], head),
            device_id_type=MESH,
        )

    def arrival(kind, way, hop, part):
        owner = seq_of(pos - hop) if way == 0 else seq_of(pos + hop)
        half = fulls[kind].shape[1] // 2
        view = fulls[kind].at[owner, pl.ds(part * half, half)]
        return pltpu.make_async_remote_copy(
            src_ref=view,
            dst_ref=view,
            send_sem=ring_send.at[kind, way, hop - 1, part],
            recv_sem=ring_recv.at[kind, way, hop - 1, part],
            device_id=(sides[way], head),
            device_id_type=MESH,
        )

    def send_first(kind):
        for part in range(2):
            for way in range(2):
                ring(kind, way, 1, part).start()

    def forward(kind, hop):
        for step in range(2):
            for way in range(2):
                part = step if way == 0 else 1 - step
                arrival(kind, way, hop, part).wait_recv()
                if step == 0:
                    ring(kind, way, hop + 1, part).start()
                else:

                    @pl.when(hop + 1 < hops)
                    def _():
                        ring(kind, way, hop + 1, part).start()

    def take_last(kind):
        for way in range(2):
            arrival(kind, way, hops, way).wait_recv()

    loads[0].wait()
    loads[1].wait()
    send_first(kv_kind)
    loads[2].wait()
    send_first(q_kinds[0])
    for load in loads[3:]:
        load.wait()

    def norm_rows(i, carry):
        rows = pl.ds(pl.multiple_of(i * 64, 64), 64)
        total = jnp.zeros((64, 1), jnp.float32)
        for b in range(n):
            x = normed[b, rows, :].astype(jnp.float32)
            total = total + jnp.sum(x * x, axis=-1, keepdims=True)
        scale = lax.rsqrt(total * (1.0 / width) + 1e-05)
        for b in range(n):
            x = normed[b, rows, :].astype(jnp.float32)
            normed[b, rows, :] = (x * scale * gain[b]).astype(jnp.bfloat16)
        return carry

    lax.fori_loop(0, token_count // 64, norm_rows, 0)

    def project(acc, columns, kind, owner, first=False):
        def body(i, carry):
            rows = pl.ds(pl.multiple_of(i * tile, tile), tile)
            product = jnp.dot(
                normed[owner, rows, :], fulls[kind][owner], preferred_element_type=jnp.float32
            )
            if first:
                acc[rows, columns] = product
            else:
                acc[rows, columns] += product
            return carry

        lax.fori_loop(0, token_count // tile, body, 0)

    def project_hop(acc, columns, kind, hop):
        def body(side, carry):
            project(acc, columns, kind, seq_of(pos - hop + 2 * hop * side))
            return carry

        lax.fori_loop(0, 2, body, 0)

    kv_columns = slice(0, 2 * kv_width)
    q_columns = [slice(part * q_part, (part + 1) * q_part) for part in range(2)]

    def middle(acc, columns, kind):
        def step(hop, carry):
            forward(kind, hop)
            project_hop(acc, columns, kind, hop - 1)
            return carry

        lax.fori_loop(3, hops, step, 0)

    project(acc_kv, kv_columns, kv_kind, me, True)
    forward(kv_kind, 1)
    project_hop(acc_kv, kv_columns, kv_kind, 1)
    forward(kv_kind, 2)
    middle(acc_kv, kv_columns, kv_kind)
    forward(q_kinds[0], 1)
    project_hop(acc_kv, kv_columns, kv_kind, hops - 1)
    take_last(kv_kind)
    project(acc_kv, kv_columns, kv_kind, seq_of(pos + hops))

    project(acc_q, q_columns[0], q_kinds[0], me, True)
    forward(q_kinds[0], 2)
    send_first(q_kinds[1])
    project_hop(acc_q, q_columns[0], q_kinds[0], 1)

    for j in range(kv_heads):
        for s in range(segments):
            rows = slice(s * SEG, (s + 1) * SEG)
            key = acc_kv[rows, j * HD : (j + 1) * HD].astype(jnp.bfloat16)
            value = acc_kv[rows, kv_width + j * HD : kv_width + (j + 1) * HD].astype(jnp.bfloat16)
            keys[j, rows, :] = key
            vals[j, rows, :] = value
            feats = feature_map(key.astype(jnp.float32))
            deltas[s, j] = jnp.dot(
                feats.T.astype(jnp.bfloat16), value, preferred_element_type=jnp.float32
            )
            delta_norms[s, j] = jnp.broadcast_to(jnp.sum(feats, axis=0, keepdims=True), (8, HD))
        own = deltas[0, j]
        own_norm = delta_norms[0, j]
        for s in range(1, segments):
            own = own + deltas[s, j]
            own_norm = own_norm + delta_norms[s, j]
        mem_full[me, j * MEM_ROWS : j * MEM_ROWS + HD, :] = own.astype(jnp.bfloat16)
        mem_full[me, j * MEM_ROWS + HD : (j + 1) * MEM_ROWS, :] = jnp.concatenate(
            [own_norm, own_norm], axis=0
        ).astype(jnp.bfloat16)
    send_first(mem_kind)

    middle(acc_q, q_columns[0], q_kinds[0])
    forward(q_kinds[1], 1)
    project_hop(acc_q, q_columns[0], q_kinds[0], hops - 1)
    take_last(q_kinds[0])
    project(acc_q, q_columns[0], q_kinds[0], seq_of(pos + hops))

    def round_queries(part):
        for h in range(part * (q_heads // 2), (part + 1) * (q_heads // 2)):
            queries[h] = acc_q[:, h * HD : (h + 1) * HD].astype(jnp.bfloat16)

    exponent_scale = LOG2E / math.sqrt(HD)
    half_seg = SEG // 2

    def scores_of(left, right):
        return lax.dot_general(
            left, right, (((1,), (1,)), ((), ())), preferred_element_type=jnp.float32
        )

    def attend(h, carry):
        j = lax.div(h, group)
        columns = pl.ds(pl.multiple_of(h * HD, HD), HD)
        at_row = lax.broadcasted_iota(jnp.int32, (half_seg, half_seg), 0)
        at_col = lax.broadcasted_iota(jnp.int32, (half_seg, half_seg), 1)
        allowed = at_row >= at_col
        for s in range(segments):
            for t in range(2):
                start = s * SEG + t * half_seg
                query = queries[h, start : start + half_seg, :]
                near_keys = keys[j, start : start + half_seg, :]
                diagonal = jnp.where(allowed, scores_of(query, near_keys), -1e30)
                peak = jnp.max(diagonal, axis=-1, keepdims=True)
                if t:
                    full = scores_of(query, keys[j, start - half_seg : start, :])
                    peak = jnp.maximum(peak, jnp.max(full, axis=-1, keepdims=True))
                expd = jnp.exp2((diagonal - peak) * exponent_scale)
                total = jnp.sum(expd, axis=-1, keepdims=True)
                summed = jnp.dot(
                    expd.astype(jnp.bfloat16),
                    vals[j, start : start + half_seg, :],
                    preferred_element_type=jnp.float32,
                )
                if t:
                    expd = jnp.exp2((full - peak) * exponent_scale)
                    total = total + jnp.sum(expd, axis=-1, keepdims=True)
                    summed = summed + jnp.dot(
                        expd.astype(jnp.bfloat16),
                        vals[j, start - half_seg : start, :],
                        preferred_element_type=jnp.float32,
                    )
                acc_q[start : start + half_seg, columns] = summed / total
        return carry

    half_heads = q_heads // 2
    round_queries(0)
    forward(q_kinds[1], 2)
    send_first(wo_kinds[0])
    forward(mem_kind, 1)
    project(acc_q, q_columns[1], q_kinds[1], me, True)
    project_hop(acc_q, q_columns[1], q_kinds[1], 1)
    lax.fori_loop(0, half_heads // 2, attend, 0)

    def q_step(hop, carry):
        forward(q_kinds[1], hop)
        forward(mem_kind, hop - 1)
        project_hop(acc_q, q_columns[1], q_kinds[1], hop - 1)
        return carry

    lax.fori_loop(3, hops, q_step, 0)
    lax.fori_loop(half_heads // 2, half_heads, attend, 0)
    forward(wo_kinds[0], 1)
    forward(mem_kind, hops - 1)
    project_hop(acc_q, q_columns[1], q_kinds[1], hops - 1)
    take_last(q_kinds[1])
    project(acc_q, q_columns[1], q_kinds[1], seq_of(pos + hops))
    round_queries(1)
    forward(wo_kinds[0], 2)
    if wo_parts > 1:
        send_first(wo_kinds[1])
    lax.fori_loop(half_heads, q_heads, attend, 0)

    def pass_on(kind):
        def step(hop, carry):
            forward(kind, hop)
            return carry

        lax.fori_loop(3, hops, step, 0)

    pass_on(wo_kinds[0])

    take_last(mem_kind)
    for j in range(kv_heads):

        def add_earlier(s, carry):
            mem, norm = carry
            earlier = mem_full[s, j * MEM_ROWS : (j + 1) * MEM_ROWS, :].astype(jnp.float32)
            return mem + earlier[:HD], norm + earlier[HD : HD + 8]

        mem, norm = lax.fori_loop(
            0,
            me,
            add_earlier,
            (mem_init[j], jnp.broadcast_to(norm_init[j], (8, HD))),
        )
        for s in range(segments):
            memory[s, j, :, :HD] = mem.astype(jnp.bfloat16)
            memory[s, j, :, HD:] = jnp.broadcast_to(norm[:1], (HD, HD)).T.astype(jnp.bfloat16)
            if s + 1 < segments:
                mem = mem + deltas[s, j]
                norm = norm + delta_norms[s, j]

    def retrieve(h, carry):
        j = lax.div(h, group)
        columns = pl.ds(pl.multiple_of(h * HD, HD), HD)
        gate = 1.0 / (1.0 + jnp.exp(-jnp.full((1, HD), gates[h], jnp.float32)))
        for s in range(segments):
            rows = slice(s * SEG, (s + 1) * SEG)
            feats = feature_map(queries[h, rows, :].astype(jnp.float32)).astype(jnp.bfloat16)
            both = jnp.dot(feats, memory[s, j], preferred_element_type=jnp.float32)
            retrieved = both[:, :HD] / both[:, HD:]
            mixed[rows, columns] = (
                gate * retrieved + (1.0 - gate) * acc_q[rows, columns]
            ).astype(jnp.bfloat16)
        return carry

    lax.fori_loop(0, q_heads, retrieve, 0)

    def place_of(c):
        target = lax.div(c, per_head)
        slot = lax.div(target, 2) * per_head + lax.rem(c, per_head)
        return target, slot

    def give(part, c):
        target, slot = place_of(c)
        return pltpu.make_async_remote_copy(
            src_ref=normed.at[c, :, pl.ds(part * sub, sub)],
            dst_ref=got.at[part, slot],
            send_sem=give_send.at[part, slot],
            recv_sem=give_recv.at[part, slot],
            device_id=(me, partner),
            device_id_type=MESH,
        )

    def cross(part, c):
        index = lax.rem(c, per_head)
        return pltpu.make_async_remote_copy(
            src_ref=normed.at[c, :, pl.ds(part * sub, sub)],
            dst_ref=xgot.at[part, index],
            send_sem=x_send.at[part, index],
            recv_sem=x_recv.at[part, index],
            device_id=(me, across),
            device_id_type=MESH,
        )

    def emit(part, c):
        columns = slice(part * sub, (part + 1) * sub)

        def body(i, carry):
            rows = pl.ds(pl.multiple_of(i * tile, tile), tile)
            normed[c, rows, columns] = jnp.dot(
                mixed[rows, :], wo_full[part, c], preferred_element_type=jnp.float32
            ).astype(jnp.bfloat16)
            return carry

        lax.fori_loop(0, token_count // tile, body, 0)
        target, slot = place_of(c)

        @pl.when(lax.rem(target, 2) != core)
        def _():
            give(part, c).start()

    def finish(part, c):
        target, slot = place_of(c)
        columns = slice(part * sub, (part + 1) * sub)

        @pl.when(lax.rem(target, 2) == core)
        def _():
            give(part, c).wait_recv()

            def body(i, carry):
                rows = pl.ds(pl.multiple_of(i * tile, tile), tile)
                normed[c, rows, columns] = (
                    normed[c, rows, columns].astype(jnp.float32)
                    + got[part, slot, rows, :].astype(jnp.float32)
                ).astype(jnp.bfloat16)
                return carry

            @pl.when(target != head)
            def _():
                lax.fori_loop(0, token_count // tile, body, 0)
                cross(part, c).start()

    def out_hops(part, first, last):
        def out_step(hop, carry):
            def emit_side(side, inner):
                emit(part, seq_of(pos - hop + 2 * hop * side))
                return inner

            def finish_side(side, inner):
                finish(part, seq_of(pos - hop + 2 * hop * side))
                return inner

            lax.fori_loop(0, 2, emit_side, 0)
            lax.fori_loop(0, 2, finish_side, 0)
            return carry

        lax.fori_loop(first, last + 1, out_step, 0)

    def out_one(part, c):
        emit(part, c)
        finish(part, c)

    def collect(part):
        for o in range(per_head):
            c = head * per_head + o
            cross(part, c).wait_recv()
            slot = lax.div(head, 2) * per_head + o
            columns = slice(part * sub, (part + 1) * sub)
            placed = slice(o * block + part * sub, o * block + (part + 1) * sub)

            def body(i, carry):
                rows = pl.ds(pl.multiple_of(i * tile, tile), tile)
                out[rows, placed] = (
                    normed[c, rows, columns].astype(jnp.float32)
                    + got[part, slot, rows, :].astype(jnp.float32)
                    + xgot[part, o, rows, :].astype(jnp.float32)
                ).astype(jnp.bfloat16)
                return carry

            lax.fori_loop(0, token_count // tile, body, 0)

    for part in range(wo_parts):
        kind = wo_kinds[part]
        more = part + 1 < wo_parts
        if more:
            forward(wo_kinds[part + 1], 1)
        out_one(part, me)
        out_hops(part, 1, hops - 2)
        if more:
            forward(wo_kinds[part + 1], 2)
        out_hops(part, hops - 1, hops - 1)
        take_last(kind)
        out_one(part, seq_of(pos + hops))
        if more:
            pass_on(wo_kinds[part + 1])
    for part in range(wo_parts):
        collect(part)

    for kind in range(len(fulls)):

        def drain(hop, carry):
            for way in range(2):
                for part in range(2):
                    ring(kind, way, hop, part).wait_send()
            return carry

        lax.fori_loop(1, hops, drain, 0)
        for way in range(2):
            ring(kind, way, hops, way).wait_send()

    def drain_out(c, carry):
        target, slot = place_of(c)
        for part in range(wo_parts):

            @pl.when(lax.rem(target, 2) != core)
            def _():
                give(part, c).wait_send()

            @pl.when((lax.rem(target, 2) == core) & (target != head))
            def _():
                cross(part, c).wait_send()

        return carry

    lax.fori_loop(0, n, drain_out, 0)


def per_device(n, heads_axis, tokens, norm_gain, wq, wk, wv, wo, gate_bias, mem_init, norm_init):
    token_count, width = tokens.shape
    rows_in = wq.shape[0]
    q_width = wq.shape[1]
    kv_width = wk.shape[1]
    q_heads = q_width // HD
    kv_heads = kv_width // HD
    block = wo.shape[1]
    segments = token_count // SEG
    hops = n // 2
    per_head = n // heads_axis
    wo_parts = 2 if block % (2 * HD) == 0 else 1
    kinds = 4 + wo_parts
    gain = norm_gain.reshape(n, 1, rows_in)
    anywhere = pl.BlockSpec(memory_space=pl.ANY)
    near = pl.BlockSpec(memory_space=pltpu.VMEM)
    scalars = pl.BlockSpec(memory_space=pltpu.SMEM)
    bf16, f32 = jnp.bfloat16, jnp.float32
    flops = 2 * token_count * (width * (q_width + 2 * kv_width) + q_width * width)
    return pl.pallas_call(
        functools.partial(layer_kernel, n, heads_axis, wo_parts),
        out_shape=jax.ShapeDtypeStruct((token_count, per_head * block), bf16),
        in_specs=[anywhere, near, anywhere, anywhere, anywhere, anywhere, scalars, near, near],
        out_specs=near,
        scratch_shapes=[
            pltpu.VMEM((n, token_count, rows_in), bf16),
            pltpu.VMEM((n, rows_in, 2 * kv_width), bf16),
            pltpu.VMEM((2, n, rows_in, q_width // 2), bf16),
            pltpu.VMEM((wo_parts, n, q_width, block // wo_parts), bf16),
            pltpu.VMEM((n, kv_heads * MEM_ROWS, HD), bf16),
            pltpu.VMEM((token_count, 2 * kv_width), f32),
            pltpu.VMEM((token_count, q_width), f32),
            pltpu.VMEM((kv_heads, token_count, HD), bf16),
            pltpu.VMEM((kv_heads, token_count, HD), bf16),
            pltpu.VMEM((q_heads, token_count, HD), bf16),
            pltpu.VMEM((segments, kv_heads, HD, HD), f32),
            pltpu.VMEM((segments, kv_heads, 8, HD), f32),
            pltpu.VMEM((segments, kv_heads, HD, 2 * HD), bf16),
            pltpu.VMEM((token_count, q_width), bf16),
            pltpu.VMEM((wo_parts, n // 2, token_count, block // wo_parts), bf16),
            pltpu.VMEM((wo_parts, per_head, token_count, block // wo_parts), bf16),
            pltpu.SemaphoreType.DMA((kinds, 2, hops, 2)),
            pltpu.SemaphoreType.DMA((kinds, 2, hops, 2)),
            pltpu.SemaphoreType.DMA((wo_parts, n // 2)),
            pltpu.SemaphoreType.DMA((wo_parts, n // 2)),
            pltpu.SemaphoreType.DMA((wo_parts, per_head)),
            pltpu.SemaphoreType.DMA((wo_parts, per_head)),
            pltpu.SemaphoreType.DMA((4 + wo_parts + n,)),
        ],
        compiler_params=pltpu.CompilerParams(
            collective_id=0, has_side_effects=True, vmem_limit_bytes=60 * 1024 * 1024
        ),
        cost_estimate=pl.CostEstimate(
            flops=flops, bytes_accessed=2 * token_count * width, transcendentals=0
        ),
    )(tokens, gain, wq, wk, wv, wo, gate_bias, mem_init, norm_init.reshape(kv_heads, 1, HD))


def solution(mesh):
    placed = (
        P("seq", None),
        P(),
        P("seq", "head"),
        P("seq", "head"),
        P("seq", "head"),
        P("head", "seq"),
        P("head"),
        P("head", None, None),
        P("head", None),
    )
    return jax.shard_map(
        functools.partial(per_device, mesh.shape["seq"], mesh.shape["head"]),
        mesh=mesh,
        in_specs=placed,
        out_specs=P("seq", "head"),
        check_vma=False,
    )
```

```python
import functools
import math

import jax
import jax.numpy as jnp
from jax import lax
from jax.experimental import pallas as pl
from jax.experimental.pallas import tpu as pltpu
from jax.sharding import PartitionSpec as P

HD = 128
SEG = 512
NORM_ROWS = 16
MEM_ROWS = HD + NORM_ROWS
MESH = pl.DeviceIdType.MESH
LOG2E = math.log2(math.e)


def feature_map(values_in):
    return jnp.where(values_in > 0, values_in + 1.0, jnp.exp(jnp.minimum(values_in, 0.0)))


def layer_kernel(
    n,
    heads_axis,
    wo_parts,
    tokens,
    gain,
    wq,
    wk,
    wv,
    wo,
    gates,
    mem_init,
    norm_init,
    out,
    normed,
    kv_full,
    q_full,
    wo_full,
    mem_full,
    acc_kv,
    acc_q,
    keys,
    vals,
    queries,
    deltas,
    delta_norms,
    memory,
    mixed,
    got,
    xgot,
    ring_send,
    ring_recv,
    give_send,
    give_recv,
    x_send,
    x_recv,
    load_sem,
):
    me = lax.axis_index("seq")
    head = lax.axis_index("head")
    hops = n // 2
    per_head = n // heads_axis
    rows_in = wq.shape[0]
    token_count = tokens.shape[0]
    kv_width = wk.shape[1]
    q_width = wq.shape[1]
    q_part = q_width // 2
    q_heads = q_width // HD
    kv_heads = kv_width // HD
    group = q_heads // kv_heads
    segments = token_count // SEG
    width = tokens.shape[1]
    block = wo.shape[1]
    sub = block // wo_parts
    tile = 256
    kv_kind, q_kinds = 0, (1, 2)
    wo_kinds = tuple(range(3, 3 + wo_parts))
    mem_kind = 3 + wo_parts

    odd = lax.rem(me, 2)
    pos = (1 - odd) * lax.div(me, 2) + odd * (n - 1 - lax.div(me, 2))

    def seq_of(place):
        place = lax.rem(place + n, n)
        far = lax.div(place, hops)
        return (1 - far) * 2 * place + far * (2 * (n - place) - 1)

    sides = (seq_of(pos + 1), seq_of(pos - 1))
    core = lax.rem(head, 2)
    partner = head + 1 - 2 * core
    across = lax.rem(head + heads_axis // 2, heads_axis)

    loads = [
        pltpu.make_async_copy(wk, kv_full.at[me, :, pl.ds(0, kv_width)], load_sem.at[0]),
        pltpu.make_async_copy(wv, kv_full.at[me, :, pl.ds(kv_width, kv_width)], load_sem.at[1]),
    ]
    for part in range(2):
        loads.append(
            pltpu.make_async_copy(
                wq.at[:, pl.ds(part * q_part, q_part)], q_full.at[part, me], load_sem.at[2 + part]
            )
        )
    for part in range(wo_parts):
        loads.append(
            pltpu.make_async_copy(
                wo.at[:, pl.ds(part * sub, sub)], wo_full.at[part, me], load_sem.at[4 + part]
            )
        )
    weight_loads = len(loads)
    for i in range(n):
        loads.append(
            pltpu.make_async_copy(
                tokens.at[:, pl.ds(i * rows_in, rows_in)], normed.at[i], load_sem.at[weight_loads + i]
            )
        )
    for load in loads:
        load.start()

    barrier = pltpu.get_barrier_semaphore()
    for side in sides:
        pl.semaphore_signal(barrier, inc=1, device_id=(side, head), device_id_type=MESH)
    for other in (partner, across):
        pl.semaphore_signal(barrier, inc=1, device_id=(me, other), device_id_type=MESH)
    pl.semaphore_wait(barrier, 4)

    fulls = [kv_full, q_full.at[0], q_full.at[1]]
    fulls += [wo_full.at[part] for part in range(wo_parts)]
    fulls.append(mem_full)

    def ring(kind, way, hop, part):
        owner = seq_of(pos - hop + 1) if way == 0 else seq_of(pos + hop - 1)
        half = fulls[kind].shape[1] // 2
        view = fulls[kind].at[owner, pl.ds(part * half, half)]
        return pltpu.make_async_remote_copy(
            src_ref=view,
            dst_ref=view,
            send_sem=ring_send.at[kind, way, hop - 1, part],
            recv_sem=ring_recv.at[kind, way, hop - 1, part],
            device_id=(sides[way], head),
            device_id_type=MESH,
        )

    def arrival(kind, way, hop, part):
        owner = seq_of(pos - hop) if way == 0 else seq_of(pos + hop)
        half = fulls[kind].shape[1] // 2
        view = fulls[kind].at[owner, pl.ds(part * half, half)]
        return pltpu.make_async_remote_copy(
            src_ref=view,
            dst_ref=view,
            send_sem=ring_send.at[kind, way, hop - 1, part],
            recv_sem=ring_recv.at[kind, way, hop - 1, part],
            device_id=(sides[way], head),
            device_id_type=MESH,
        )

    def send_first(kind):
        for part in range(2):
            for way in range(2):
                ring(kind, way, 1, part).start()

    def forward(kind, hop):
        for step in range(2):
            for way in range(2):
                part = step if way == 0 else 1 - step
                arrival(kind, way, hop, part).wait_recv()
                if step == 0:
                    ring(kind, way, hop + 1, part).start()
                else:

                    @pl.when(hop + 1 < hops)
                    def _():
                        ring(kind, way, hop + 1, part).start()

    def take_last(kind):
        for way in range(2):
            arrival(kind, way, hops, way).wait_recv()

    loads[0].wait()
    loads[1].wait()
    send_first(kv_kind)
    loads[2].wait()
    send_first(q_kinds[0])
    for load in loads[3:]:
        load.wait()

    def norm_rows(i, carry):
        rows = pl.ds(pl.multiple_of(i * 64, 64), 64)
        total = jnp.zeros((64, 1), jnp.float32)
        for b in range(n):
            x = normed[b, rows, :].astype(jnp.float32)
            total = total + jnp.sum(x * x, axis=-1, keepdims=True)
        scale = lax.rsqrt(total * (1.0 / width) + 1e-05)
        for b in range(n):
            x = normed[b, rows, :].astype(jnp.float32)
            normed[b, rows, :] = (x * scale * gain[b]).astype(jnp.bfloat16)
        return carry

    lax.fori_loop(0, token_count // 64, norm_rows, 0)

    def project(acc, columns, kind, owner, first=False):
        def body(i, carry):
            rows = pl.ds(pl.multiple_of(i * tile, tile), tile)
            product = jnp.dot(
                normed[owner, rows, :], fulls[kind][owner], preferred_element_type=jnp.float32
            )
            if first:
                acc[rows, columns] = product
            else:
                acc[rows, columns] += product
            return carry

        lax.fori_loop(0, token_count // tile, body, 0)

    def project_hop(acc, columns, kind, hop):
        def body(side, carry):
            project(acc, columns, kind, seq_of(pos - hop + 2 * hop * side))
            return carry

        lax.fori_loop(0, 2, body, 0)

    kv_columns = slice(0, 2 * kv_width)
    q_columns = [slice(part * q_part, (part + 1) * q_part) for part in range(2)]

    def middle(acc, columns, kind):
        def step(hop, carry):
            forward(kind, hop)
            project_hop(acc, columns, kind, hop - 1)
            return carry

        lax.fori_loop(3, hops, step, 0)

    project(acc_kv, kv_columns, kv_kind, me, True)
    forward(kv_kind, 1)
    project_hop(acc_kv, kv_columns, kv_kind, 1)
    forward(kv_kind, 2)
    forward(q_kinds[0], 1)
    middle(acc_kv, kv_columns, kv_kind)
    send_first(q_kinds[1])
    project_hop(acc_kv, kv_columns, kv_kind, hops - 1)
    take_last(kv_kind)
    project(acc_kv, kv_columns, kv_kind, seq_of(pos + hops))

    project(acc_q, q_columns[0], q_kinds[0], me, True)
    forward(q_kinds[0], 2)
    project_hop(acc_q, q_columns[0], q_kinds[0], 1)

    for j in range(kv_heads):
        for s in range(segments):
            rows = slice(s * SEG, (s + 1) * SEG)
            key = acc_kv[rows, j * HD : (j + 1) * HD].astype(jnp.bfloat16)
            value = acc_kv[rows, kv_width + j * HD : kv_width + (j + 1) * HD].astype(jnp.bfloat16)
            keys[j, rows, :] = key
            vals[j, rows, :] = value
            feats = feature_map(key.astype(jnp.float32))
            deltas[s, j] = jnp.dot(
                feats.T.astype(jnp.bfloat16), value, preferred_element_type=jnp.float32
            )
            delta_norms[s, j] = jnp.broadcast_to(jnp.sum(feats, axis=0, keepdims=True), (8, HD))
        own = deltas[0, j]
        own_norm = delta_norms[0, j]
        for s in range(1, segments):
            own = own + deltas[s, j]
            own_norm = own_norm + delta_norms[s, j]
        mem_full[me, j * MEM_ROWS : j * MEM_ROWS + HD, :] = own.astype(jnp.bfloat16)
        mem_full[me, j * MEM_ROWS + HD : (j + 1) * MEM_ROWS, :] = jnp.concatenate(
            [own_norm, own_norm], axis=0
        ).astype(jnp.bfloat16)
    send_first(mem_kind)

    forward(q_kinds[1], 1)
    middle(acc_q, q_columns[0], q_kinds[0])
    send_first(wo_kinds[0])
    project_hop(acc_q, q_columns[0], q_kinds[0], hops - 1)
    take_last(q_kinds[0])
    project(acc_q, q_columns[0], q_kinds[0], seq_of(pos + hops))

    def round_queries(part):
        for h in range(part * (q_heads // 2), (part + 1) * (q_heads // 2)):
            queries[h] = acc_q[:, h * HD : (h + 1) * HD].astype(jnp.bfloat16)

    exponent_scale = LOG2E / math.sqrt(HD)
    half_seg = SEG // 2

    def scores_of(left, right):
        return lax.dot_general(
            left, right, (((1,), (1,)), ((), ())), preferred_element_type=jnp.float32
        )

    def attend(h, carry):
        j = lax.div(h, group)
        columns = pl.ds(pl.multiple_of(h * HD, HD), HD)
        at_row = lax.broadcasted_iota(jnp.int32, (half_seg, half_seg), 0)
        at_col = lax.broadcasted_iota(jnp.int32, (half_seg, half_seg), 1)
        allowed = at_row >= at_col
        for s in range(segments):
            for t in range(2):
                start = s * SEG + t * half_seg
                query = queries[h, start : start + half_seg, :]
                near_keys = keys[j, start : start + half_seg, :]
                diagonal = jnp.where(allowed, scores_of(query, near_keys), -1e30)
                peak = jnp.max(diagonal, axis=-1, keepdims=True)
                if t:
                    full = scores_of(query, keys[j, start - half_seg : start, :])
                    peak = jnp.maximum(peak, jnp.max(full, axis=-1, keepdims=True))
                expd = jnp.exp2((diagonal - peak) * exponent_scale)
                total = jnp.sum(expd, axis=-1, keepdims=True)
                summed = jnp.dot(
                    expd.astype(jnp.bfloat16),
                    vals[j, start : start + half_seg, :],
                    preferred_element_type=jnp.float32,
                )
                if t:
                    expd = jnp.exp2((full - peak) * exponent_scale)
                    total = total + jnp.sum(expd, axis=-1, keepdims=True)
                    summed = summed + jnp.dot(
                        expd.astype(jnp.bfloat16),
                        vals[j, start - half_seg : start, :],
                        preferred_element_type=jnp.float32,
                    )
                acc_q[start : start + half_seg, columns] = summed / total
        return carry

    half_heads = q_heads // 2
    round_queries(0)
    forward(q_kinds[1], 2)
    project(acc_q, q_columns[1], q_kinds[1], me, True)
    project_hop(acc_q, q_columns[1], q_kinds[1], 1)
    forward(mem_kind, 1)
    lax.fori_loop(0, half_heads // 2, attend, 0)
    forward(wo_kinds[0], 1)

    def q_step(hop, carry):
        forward(q_kinds[1], hop)
        forward(mem_kind, hop - 1)
        project_hop(acc_q, q_columns[1], q_kinds[1], hop - 1)
        return carry

    lax.fori_loop(3, hops, q_step, 0)
    if wo_parts > 1:
        send_first(wo_kinds[1])
    lax.fori_loop(half_heads // 2, half_heads, attend, 0)
    project_hop(acc_q, q_columns[1], q_kinds[1], hops - 1)
    take_last(q_kinds[1])
    project(acc_q, q_columns[1], q_kinds[1], seq_of(pos + hops))
    round_queries(1)
    lax.fori_loop(half_heads, half_heads + half_heads // 2, attend, 0)
    forward(wo_kinds[0], 2)
    forward(mem_kind, hops - 1)
    lax.fori_loop(half_heads + half_heads // 2, q_heads, attend, 0)
    if wo_parts > 1:
        forward(wo_kinds[1], 1)

    take_last(mem_kind)
    for j in range(kv_heads):

        def add_earlier(s, carry):
            mem, norm = carry
            earlier = mem_full[s, j * MEM_ROWS : (j + 1) * MEM_ROWS, :].astype(jnp.float32)
            return mem + earlier[:HD], norm + earlier[HD : HD + 8]

        mem, norm = lax.fori_loop(
            0,
            me,
            add_earlier,
            (mem_init[j], jnp.broadcast_to(norm_init[j], (8, HD))),
        )
        for s in range(segments):
            memory[s, j, :, :HD] = mem.astype(jnp.bfloat16)
            memory[s, j, :, HD:] = jnp.broadcast_to(norm[:1], (HD, HD)).T.astype(jnp.bfloat16)
            if s + 1 < segments:
                mem = mem + deltas[s, j]
                norm = norm + delta_norms[s, j]

    def retrieve(h, carry):
        j = lax.div(h, group)
        columns = pl.ds(pl.multiple_of(h * HD, HD), HD)
        gate = 1.0 / (1.0 + jnp.exp(-jnp.full((1, HD), gates[h], jnp.float32)))
        for s in range(segments):
            rows = slice(s * SEG, (s + 1) * SEG)
            feats = feature_map(queries[h, rows, :].astype(jnp.float32)).astype(jnp.bfloat16)
            both = jnp.dot(feats, memory[s, j], preferred_element_type=jnp.float32)
            retrieved = both[:, :HD] / both[:, HD:]
            mixed[rows, columns] = (
                gate * retrieved + (1.0 - gate) * acc_q[rows, columns]
            ).astype(jnp.bfloat16)
        return carry

    lax.fori_loop(0, q_heads, retrieve, 0)

    def place_of(c):
        target = lax.div(c, per_head)
        slot = lax.div(target, 2) * per_head + lax.rem(c, per_head)
        return target, slot

    def give(part, c):
        target, slot = place_of(c)
        return pltpu.make_async_remote_copy(
            src_ref=normed.at[c, :, pl.ds(part * sub, sub)],
            dst_ref=got.at[part, slot],
            send_sem=give_send.at[part, slot],
            recv_sem=give_recv.at[part, slot],
            device_id=(me, partner),
            device_id_type=MESH,
        )

    def cross(part, c):
        index = lax.rem(c, per_head)
        return pltpu.make_async_remote_copy(
            src_ref=normed.at[c, :, pl.ds(part * sub, sub)],
            dst_ref=xgot.at[part, index],
            send_sem=x_send.at[part, index],
            recv_sem=x_recv.at[part, index],
            device_id=(me, across),
            device_id_type=MESH,
        )

    def emit(part, c):
        columns = slice(part * sub, (part + 1) * sub)

        def body(i, carry):
            rows = pl.ds(pl.multiple_of(i * tile, tile), tile)
            normed[c, rows, columns] = jnp.dot(
                mixed[rows, :], wo_full[part, c], preferred_element_type=jnp.float32
            ).astype(jnp.bfloat16)
            return carry

        lax.fori_loop(0, token_count // tile, body, 0)
        target, slot = place_of(c)

        @pl.when(lax.rem(target, 2) != core)
        def _():
            give(part, c).start()

    def finish(part, c):
        target, slot = place_of(c)
        columns = slice(part * sub, (part + 1) * sub)

        @pl.when(lax.rem(target, 2) == core)
        def _():
            give(part, c).wait_recv()

            def body(i, carry):
                rows = pl.ds(pl.multiple_of(i * tile, tile), tile)
                normed[c, rows, columns] = (
                    normed[c, rows, columns].astype(jnp.float32)
                    + got[part, slot, rows, :].astype(jnp.float32)
                ).astype(jnp.bfloat16)
                return carry

            @pl.when(target != head)
            def _():
                lax.fori_loop(0, token_count // tile, body, 0)
                cross(part, c).start()

    def each_block(work, part, hop):
        def side_step(side, carry):
            work(part, seq_of(pos - hop + 2 * hop * side))
            return carry

        lax.fori_loop(0, 2 - lax.div(1, hop + 1), side_step, 0)

    def emits(part, hop):
        each_block(emit, part, hop)

    def finishes(part, hop):
        each_block(finish, part, hop)

    def collect(part):
        for o in range(per_head):
            c = head * per_head + o
            cross(part, c).wait_recv()
            slot = lax.div(head, 2) * per_head + o
            columns = slice(part * sub, (part + 1) * sub)
            placed = slice(o * block + part * sub, o * block + (part + 1) * sub)

            def body(i, carry):
                rows = pl.ds(pl.multiple_of(i * tile, tile), tile)
                out[rows, placed] = (
                    normed[c, rows, columns].astype(jnp.float32)
                    + got[part, slot, rows, :].astype(jnp.float32)
                    + xgot[part, o, rows, :].astype(jnp.float32)
                ).astype(jnp.bfloat16)
                return carry

            lax.fori_loop(0, token_count // tile, body, 0)

    last_owner = seq_of(pos + hops)
    two = wo_parts > 1
    first_kind, second_kind = wo_kinds[0], wo_kinds[-1]
    emit(0, me)
    if two:
        emit(1, me)
    finish(0, me)

    def out_step(hop, carry):
        forward(first_kind, hop)
        emits(0, hop - 2)
        if two:
            finishes(1, hop - 3)
            forward(second_kind, hop - 1)
            emits(1, hop - 2)
        finishes(0, hop - 2)
        return carry

    lax.fori_loop(3, hops, out_step, 0)
    emits(0, jnp.int32(hops - 2))
    if two:
        finishes(1, jnp.int32(hops - 3))
        forward(second_kind, hops - 1)
        emits(1, jnp.int32(hops - 2))
    finishes(0, jnp.int32(hops - 2))
    emits(0, jnp.int32(hops - 1))
    if two:
        finishes(1, jnp.int32(hops - 2))
    take_last(first_kind)
    emit(0, last_owner)
    finishes(0, jnp.int32(hops - 1))
    if two:
        emits(1, jnp.int32(hops - 1))
        finish(0, last_owner)
        finishes(1, jnp.int32(hops - 1))
        take_last(second_kind)
        emit(1, last_owner)
        finish(1, last_owner)
    else:
        finish(0, last_owner)
    for part in range(wo_parts):
        collect(part)

    for kind in range(len(fulls)):

        def drain(hop, carry):
            for way in range(2):
                for part in range(2):
                    ring(kind, way, hop, part).wait_send()
            return carry

        lax.fori_loop(1, hops, drain, 0)
        for way in range(2):
            ring(kind, way, hops, way).wait_send()

    def drain_out(c, carry):
        target, slot = place_of(c)
        for part in range(wo_parts):

            @pl.when(lax.rem(target, 2) != core)
            def _():
                give(part, c).wait_send()

            @pl.when((lax.rem(target, 2) == core) & (target != head))
            def _():
                cross(part, c).wait_send()

        return carry

    lax.fori_loop(0, n, drain_out, 0)


def per_device(n, heads_axis, tokens, norm_gain, wq, wk, wv, wo, gate_bias, mem_init, norm_init):
    token_count, width = tokens.shape
    rows_in = wq.shape[0]
    q_width = wq.shape[1]
    kv_width = wk.shape[1]
    q_heads = q_width // HD
    kv_heads = kv_width // HD
    block = wo.shape[1]
    segments = token_count // SEG
    hops = n // 2
    per_head = n // heads_axis
    wo_parts = 2 if block % (2 * HD) == 0 else 1
    kinds = 4 + wo_parts
    gain = norm_gain.reshape(n, 1, rows_in)
    anywhere = pl.BlockSpec(memory_space=pl.ANY)
    near = pl.BlockSpec(memory_space=pltpu.VMEM)
    scalars = pl.BlockSpec(memory_space=pltpu.SMEM)
    bf16, f32 = jnp.bfloat16, jnp.float32
    flops = 2 * token_count * (width * (q_width + 2 * kv_width) + q_width * width)
    return pl.pallas_call(
        functools.partial(layer_kernel, n, heads_axis, wo_parts),
        out_shape=jax.ShapeDtypeStruct((token_count, per_head * block), bf16),
        in_specs=[anywhere, near, anywhere, anywhere, anywhere, anywhere, scalars, near, near],
        out_specs=near,
        scratch_shapes=[
            pltpu.VMEM((n, token_count, rows_in), bf16),
            pltpu.VMEM((n, rows_in, 2 * kv_width), bf16),
            pltpu.VMEM((2, n, rows_in, q_width // 2), bf16),
            pltpu.VMEM((wo_parts, n, q_width, block // wo_parts), bf16),
            pltpu.VMEM((n, kv_heads * MEM_ROWS, HD), bf16),
            pltpu.VMEM((token_count, 2 * kv_width), f32),
            pltpu.VMEM((token_count, q_width), f32),
            pltpu.VMEM((kv_heads, token_count, HD), bf16),
            pltpu.VMEM((kv_heads, token_count, HD), bf16),
            pltpu.VMEM((q_heads, token_count, HD), bf16),
            pltpu.VMEM((segments, kv_heads, HD, HD), f32),
            pltpu.VMEM((segments, kv_heads, 8, HD), f32),
            pltpu.VMEM((segments, kv_heads, HD, 2 * HD), bf16),
            pltpu.VMEM((token_count, q_width), bf16),
            pltpu.VMEM((wo_parts, n // 2, token_count, block // wo_parts), bf16),
            pltpu.VMEM((wo_parts, per_head, token_count, block // wo_parts), bf16),
            pltpu.SemaphoreType.DMA((kinds, 2, hops, 2)),
            pltpu.SemaphoreType.DMA((kinds, 2, hops, 2)),
            pltpu.SemaphoreType.DMA((wo_parts, n // 2)),
            pltpu.SemaphoreType.DMA((wo_parts, n // 2)),
            pltpu.SemaphoreType.DMA((wo_parts, per_head)),
            pltpu.SemaphoreType.DMA((wo_parts, per_head)),
            pltpu.SemaphoreType.DMA((4 + wo_parts + n,)),
        ],
        compiler_params=pltpu.CompilerParams(
            collective_id=0, has_side_effects=True, vmem_limit_bytes=60 * 1024 * 1024
        ),
        cost_estimate=pl.CostEstimate(
            flops=flops, bytes_accessed=2 * token_count * width, transcendentals=0
        ),
    )(tokens, gain, wq, wk, wv, wo, gate_bias, mem_init, norm_init.reshape(kv_heads, 1, HD))


def solution(mesh):
    placed = (
        P("seq", None),
        P(),
        P("seq", "head"),
        P("seq", "head"),
        P("seq", "head"),
        P("head", "seq"),
        P("head"),
        P("head", None, None),
        P("head", None),
    )
    return jax.shard_map(
        functools.partial(per_device, mesh.shape["seq"], mesh.shape["head"]),
        mesh=mesh,
        in_specs=placed,
        out_specs=P("seq", "head"),
        check_vma=False,
    )
```

```python
import functools
import math

import jax
import jax.numpy as jnp
from jax import lax
from jax.experimental import pallas as pl
from jax.experimental.pallas import tpu as pltpu
from jax.sharding import PartitionSpec as P

HD = 128
SEG = 512
NORM_ROWS = 16
MEM_ROWS = HD + NORM_ROWS
MESH = pl.DeviceIdType.MESH
LOG2E = math.log2(math.e)


def feature_map(values_in):
    return jnp.where(values_in > 0, values_in + 1.0, jnp.exp(jnp.minimum(values_in, 0.0)))


def layer_kernel(
    n,
    heads_axis,
    wo_parts,
    tokens,
    gain,
    wq,
    wk,
    wv,
    wo,
    gates,
    mem_init,
    norm_init,
    out,
    normed,
    kv_full,
    q_full,
    wo_full,
    mem_full,
    acc_kv,
    acc_q,
    keys,
    vals,
    queries,
    deltas,
    delta_norms,
    memory,
    mixed,
    got,
    xgot,
    ring_send,
    ring_recv,
    give_send,
    give_recv,
    x_send,
    x_recv,
    load_sem,
):
    me = lax.axis_index("seq")
    head = lax.axis_index("head")
    hops = n // 2
    per_head = n // heads_axis
    rows_in = wq.shape[0]
    token_count = tokens.shape[0]
    kv_width = wk.shape[1]
    q_width = wq.shape[1]
    q_part = q_width // 2
    q_heads = q_width // HD
    kv_heads = kv_width // HD
    group = q_heads // kv_heads
    segments = token_count // SEG
    width = tokens.shape[1]
    block = wo.shape[1]
    sub = block // wo_parts
    tile = 256
    kv_kind, q_kind, wo_kind, mem_kind = range(4)

    odd = lax.rem(me, 2)
    pos = (1 - odd) * lax.div(me, 2) + odd * (n - 1 - lax.div(me, 2))

    def seq_of(place):
        place = lax.rem(place + n, n)
        far = lax.div(place, hops)
        return (1 - far) * 2 * place + far * (2 * (n - place) - 1)

    sides = (seq_of(pos + 1), seq_of(pos - 1))
    core = lax.rem(head, 2)
    partner = head + 1 - 2 * core
    across = lax.rem(head + heads_axis // 2, heads_axis)

    loads = [
        pltpu.make_async_copy(wk, kv_full.at[me, :, pl.ds(0, kv_width)], load_sem.at[0]),
        pltpu.make_async_copy(wv, kv_full.at[me, :, pl.ds(kv_width, kv_width)], load_sem.at[1]),
    ]
    for part in range(2):
        loads.append(
            pltpu.make_async_copy(
                wq.at[:, pl.ds(part * q_part, q_part)], q_full.at[me, part], load_sem.at[2 + part]
            )
        )
    for part in range(wo_parts):
        loads.append(
            pltpu.make_async_copy(
                wo.at[:, pl.ds(part * sub, sub)], wo_full.at[me, part], load_sem.at[4 + part]
            )
        )
    weight_loads = len(loads)
    for i in range(n):
        loads.append(
            pltpu.make_async_copy(
                tokens.at[:, pl.ds(i * rows_in, rows_in)], normed.at[i], load_sem.at[weight_loads + i]
            )
        )
    for load in loads:
        load.start()

    barrier = pltpu.get_barrier_semaphore()
    for side in sides:
        pl.semaphore_signal(barrier, inc=1, device_id=(side, head), device_id_type=MESH)
    for other in (partner, across):
        pl.semaphore_signal(barrier, inc=1, device_id=(me, other), device_id_type=MESH)
    pl.semaphore_wait(barrier, 4)

    fulls = (kv_full, q_full, wo_full, mem_full)

    def part_of(kind, owner, part):
        if kind == q_kind or (kind == wo_kind and wo_parts == 2):
            return fulls[kind].at[owner, part]
        whole = fulls[kind].at[owner, 0] if kind == wo_kind else fulls[kind].at[owner]
        half = whole.shape[0] // 2
        return whole.at[pl.ds(part * half, half)]

    def ring(kind, way, hop, part):
        owner = seq_of(pos - hop + 1) if way == 0 else seq_of(pos + hop - 1)
        view = part_of(kind, owner, part)
        return pltpu.make_async_remote_copy(
            src_ref=view,
            dst_ref=view,
            send_sem=ring_send.at[kind, way, hop - 1, part],
            recv_sem=ring_recv.at[kind, way, hop - 1, part],
            device_id=(sides[way], head),
            device_id_type=MESH,
        )

    def arrival(kind, way, hop, part):
        owner = seq_of(pos - hop) if way == 0 else seq_of(pos + hop)
        view = part_of(kind, owner, part)
        return pltpu.make_async_remote_copy(
            src_ref=view,
            dst_ref=view,
            send_sem=ring_send.at[kind, way, hop - 1, part],
            recv_sem=ring_recv.at[kind, way, hop - 1, part],
            device_id=(sides[way], head),
            device_id_type=MESH,
        )

    def send_first(kind):
        for part in range(2):
            for way in range(2):
                ring(kind, way, 1, part).start()

    def forward(kind, hop):
        for step in range(2):
            for way in range(2):
                part = step if way == 0 else 1 - step
                arrival(kind, way, hop, part).wait_recv()
                if step == 0:
                    ring(kind, way, hop + 1, part).start()
                else:

                    @pl.when(hop + 1 < hops)
                    def _():
                        ring(kind, way, hop + 1, part).start()

    def take_last(kind):
        for way in range(2):
            arrival(kind, way, hops, way).wait_recv()

    loads[0].wait()
    loads[1].wait()
    send_first(kv_kind)
    loads[2].wait()
    loads[3].wait()
    send_first(q_kind)
    for load in loads[4:]:
        load.wait()

    def norm_rows(i, carry):
        rows = pl.ds(pl.multiple_of(i * 64, 64), 64)
        total = jnp.zeros((64, 1), jnp.float32)
        for b in range(n):
            x = normed[b, rows, :].astype(jnp.float32)
            total = total + jnp.sum(x * x, axis=-1, keepdims=True)
        scale = lax.rsqrt(total * (1.0 / width) + 1e-05)
        for b in range(n):
            x = normed[b, rows, :].astype(jnp.float32)
            normed[b, rows, :] = (x * scale * gain[b]).astype(jnp.bfloat16)
        return carry

    lax.fori_loop(0, token_count // 64, norm_rows, 0)

    def project(acc, kind, owner, first=False):
        def body(i, carry):
            rows = pl.ds(pl.multiple_of(i * tile, tile), tile)
            for part in range(2 if kind == q_kind else 1):
                weights = fulls[kind][owner, part] if kind == q_kind else fulls[kind][owner]
                span = weights.shape[-1]
                columns = slice(part * span, (part + 1) * span)
                product = jnp.dot(
                    normed[owner, rows, :], weights, preferred_element_type=jnp.float32
                )
                if first:
                    acc[rows, columns] = product
                else:
                    acc[rows, columns] += product
            return carry

        lax.fori_loop(0, token_count // tile, body, 0)

    def project_hop(acc, kind, hop):
        def body(side, carry):
            project(acc, kind, seq_of(pos - hop + 2 * hop * side))
            return carry

        lax.fori_loop(0, 2, body, 0)

    project(acc_kv, kv_kind, me, True)

    def kv_step(hop, carry):
        forward(kv_kind, hop)
        project_hop(acc_kv, kv_kind, hop)
        return carry

    lax.fori_loop(1, hops, kv_step, 0)
    take_last(kv_kind)
    forward(q_kind, 1)
    project(acc_kv, kv_kind, seq_of(pos + hops))

    for j in range(kv_heads):
        for s in range(segments):
            rows = slice(s * SEG, (s + 1) * SEG)
            key = acc_kv[rows, j * HD : (j + 1) * HD].astype(jnp.bfloat16)
            value = acc_kv[rows, kv_width + j * HD : kv_width + (j + 1) * HD].astype(jnp.bfloat16)
            keys[j, rows, :] = key
            vals[j, rows, :] = value
            feats = feature_map(key.astype(jnp.float32))
            deltas[s, j] = jnp.dot(
                feats.T.astype(jnp.bfloat16), value, preferred_element_type=jnp.float32
            )
            delta_norms[s, j] = jnp.broadcast_to(jnp.sum(feats, axis=0, keepdims=True), (8, HD))
        own = deltas[0, j]
        own_norm = delta_norms[0, j]
        for s in range(1, segments):
            own = own + deltas[s, j]
            own_norm = own_norm + delta_norms[s, j]
        mem_full[me, j * MEM_ROWS : j * MEM_ROWS + HD, :] = own.astype(jnp.bfloat16)
        mem_full[me, j * MEM_ROWS + HD : (j + 1) * MEM_ROWS, :] = jnp.concatenate(
            [own_norm, own_norm], axis=0
        ).astype(jnp.bfloat16)
    send_first(mem_kind)

    project(acc_q, q_kind, me, True)
    project_hop(acc_q, q_kind, 1)

    def q_step(hop, carry):
        forward(q_kind, hop)
        forward(mem_kind, hop - 1)
        project_hop(acc_q, q_kind, hop)
        return carry

    lax.fori_loop(2, hops, q_step, 0)
    send_first(wo_kind)
    forward(mem_kind, hops - 1)
    take_last(q_kind)
    project(acc_q, q_kind, seq_of(pos + hops))
    for h in range(q_heads):
        queries[h] = acc_q[:, h * HD : (h + 1) * HD].astype(jnp.bfloat16)

    exponent_scale = LOG2E / math.sqrt(HD)
    half_seg = SEG // 2

    def scores_of(left, right):
        return lax.dot_general(
            left, right, (((1,), (1,)), ((), ())), preferred_element_type=jnp.float32
        )

    def attend(h, carry):
        j = lax.div(h, group)
        columns = pl.ds(pl.multiple_of(h * HD, HD), HD)
        at_row = lax.broadcasted_iota(jnp.int32, (half_seg, half_seg), 0)
        at_col = lax.broadcasted_iota(jnp.int32, (half_seg, half_seg), 1)
        allowed = at_row >= at_col
        for s in range(segments):
            for t in range(2):
                start = s * SEG + t * half_seg
                query = queries[h, start : start + half_seg, :]
                near_keys = keys[j, start : start + half_seg, :]
                diagonal = jnp.where(allowed, scores_of(query, near_keys), -1e30)
                peak = jnp.max(diagonal, axis=-1, keepdims=True)
                if t:
                    full = scores_of(query, keys[j, start - half_seg : start, :])
                    peak = jnp.maximum(peak, jnp.max(full, axis=-1, keepdims=True))
                expd = jnp.exp2((diagonal - peak) * exponent_scale)
                total = jnp.sum(expd, axis=-1, keepdims=True)
                summed = jnp.dot(
                    expd.astype(jnp.bfloat16),
                    vals[j, start : start + half_seg, :],
                    preferred_element_type=jnp.float32,
                )
                if t:
                    expd = jnp.exp2((full - peak) * exponent_scale)
                    total = total + jnp.sum(expd, axis=-1, keepdims=True)
                    summed = summed + jnp.dot(
                        expd.astype(jnp.bfloat16),
                        vals[j, start - half_seg : start, :],
                        preferred_element_type=jnp.float32,
                    )
                acc_q[start : start + half_seg, columns] = summed / total
        return carry

    lax.fori_loop(0, q_heads // 2, attend, 0)
    forward(wo_kind, 1)
    lax.fori_loop(q_heads // 2, q_heads, attend, 0)

    take_last(mem_kind)
    for j in range(kv_heads):

        def add_earlier(s, carry):
            mem, norm = carry
            earlier = mem_full[s, j * MEM_ROWS : (j + 1) * MEM_ROWS, :].astype(jnp.float32)
            return mem + earlier[:HD], norm + earlier[HD : HD + 8]

        mem, norm = lax.fori_loop(
            0,
            me,
            add_earlier,
            (mem_init[j], jnp.broadcast_to(norm_init[j], (8, HD))),
        )
        for s in range(segments):
            memory[s, j, :, :HD] = mem.astype(jnp.bfloat16)
            memory[s, j, :, HD:] = jnp.broadcast_to(norm[:1], (HD, HD)).T.astype(jnp.bfloat16)
            if s + 1 < segments:
                mem = mem + deltas[s, j]
                norm = norm + delta_norms[s, j]

    def retrieve(h, carry):
        j = lax.div(h, group)
        columns = pl.ds(pl.multiple_of(h * HD, HD), HD)
        gate = 1.0 / (1.0 + jnp.exp(-jnp.full((1, HD), gates[h], jnp.float32)))
        for s in range(segments):
            rows = slice(s * SEG, (s + 1) * SEG)
            feats = feature_map(queries[h, rows, :].astype(jnp.float32)).astype(jnp.bfloat16)
            both = jnp.dot(feats, memory[s, j], preferred_element_type=jnp.float32)
            retrieved = both[:, :HD] / both[:, HD:]
            mixed[rows, columns] = (
                gate * retrieved + (1.0 - gate) * acc_q[rows, columns]
            ).astype(jnp.bfloat16)
        return carry

    lax.fori_loop(0, q_heads, retrieve, 0)

    def place_of(c):
        target = lax.div(c, per_head)
        slot = lax.div(target, 2) * per_head + lax.rem(c, per_head)
        return target, slot

    def give(part, c):
        target, slot = place_of(c)
        return pltpu.make_async_remote_copy(
            src_ref=normed.at[c, :, pl.ds(part * sub, sub)],
            dst_ref=got.at[part, slot],
            send_sem=give_send.at[part, slot],
            recv_sem=give_recv.at[part, slot],
            device_id=(me, partner),
            device_id_type=MESH,
        )

    def cross(part, c):
        index = lax.rem(c, per_head)
        return pltpu.make_async_remote_copy(
            src_ref=normed.at[c, :, pl.ds(part * sub, sub)],
            dst_ref=xgot.at[part, index],
            send_sem=x_send.at[part, index],
            recv_sem=x_recv.at[part, index],
            device_id=(me, across),
            device_id_type=MESH,
        )

    def emit(part, c):
        columns = slice(part * sub, (part + 1) * sub)

        def body(i, carry):
            rows = pl.ds(pl.multiple_of(i * tile, tile), tile)
            normed[c, rows, columns] = jnp.dot(
                mixed[rows, :], wo_full[c, part], preferred_element_type=jnp.float32
            ).astype(jnp.bfloat16)
            return carry

        lax.fori_loop(0, token_count // tile, body, 0)
        target, slot = place_of(c)

        @pl.when(lax.rem(target, 2) != core)
        def _():
            give(part, c).start()

    def finish(part, c):
        target, slot = place_of(c)
        columns = slice(part * sub, (part + 1) * sub)

        @pl.when(lax.rem(target, 2) == core)
        def _():
            give(part, c).wait_recv()

            def body(i, carry):
                rows = pl.ds(pl.multiple_of(i * tile, tile), tile)
                normed[c, rows, columns] = (
                    normed[c, rows, columns].astype(jnp.float32)
                    + got[part, slot, rows, :].astype(jnp.float32)
                ).astype(jnp.bfloat16)
                return carry

            @pl.when(target != head)
            def _():
                lax.fori_loop(0, token_count // tile, body, 0)
                cross(part, c).start()

    def each_block(work, part, hop):
        def side_step(side, carry):
            work(part, seq_of(pos - hop + 2 * hop * side))
            return carry

        lax.fori_loop(0, 2 - lax.div(1, hop + 1), side_step, 0)

    def emits(hop):
        for part in range(wo_parts):
            each_block(emit, part, hop)

    def finishes(hop):
        for part in range(wo_parts):
            each_block(finish, part, hop)

    def collect(part):
        for o in range(per_head):
            c = head * per_head + o
            cross(part, c).wait_recv()
            slot = lax.div(head, 2) * per_head + o
            columns = slice(part * sub, (part + 1) * sub)
            placed = slice(o * block + part * sub, o * block + (part + 1) * sub)

            def body(i, carry):
                rows = pl.ds(pl.multiple_of(i * tile, tile), tile)
                out[rows, placed] = (
                    normed[c, rows, columns].astype(jnp.float32)
                    + got[part, slot, rows, :].astype(jnp.float32)
                    + xgot[part, o, rows, :].astype(jnp.float32)
                ).astype(jnp.bfloat16)
                return carry

            lax.fori_loop(0, token_count // tile, body, 0)

    last_owner = seq_of(pos + hops)
    emits(jnp.int32(0))
    forward(wo_kind, 2)
    emits(jnp.int32(1))
    finishes(jnp.int32(0))
    emits(jnp.int32(2))
    finishes(jnp.int32(1))

    def out_step(hop, carry):
        finishes(hop - 1)
        forward(wo_kind, hop)
        emits(hop)
        return carry

    lax.fori_loop(3, hops, out_step, 0)
    if wo_parts == 2:
        finishes(jnp.int32(hops - 1))
        for way in range(2):
            arrival(wo_kind, way, hops, way).wait_recv()
            emit(way, last_owner)
        for way in range(2):
            finish(way, last_owner)
    else:
        take_last(wo_kind)
        emit(0, last_owner)
        finishes(jnp.int32(hops - 1))
        finish(0, last_owner)
    for part in range(wo_parts):
        collect(part)

    for kind in range(len(fulls)):

        def drain(hop, carry):
            for way in range(2):
                for part in range(2):
                    ring(kind, way, hop, part).wait_send()
            return carry

        lax.fori_loop(1, hops, drain, 0)
        for way in range(2):
            ring(kind, way, hops, way).wait_send()

    def drain_out(c, carry):
        target, slot = place_of(c)
        for part in range(wo_parts):

            @pl.when(lax.rem(target, 2) != core)
            def _():
                give(part, c).wait_send()

            @pl.when((lax.rem(target, 2) == core) & (target != head))
            def _():
                cross(part, c).wait_send()

        return carry

    lax.fori_loop(0, n, drain_out, 0)


def per_device(n, heads_axis, tokens, norm_gain, wq, wk, wv, wo, gate_bias, mem_init, norm_init):
    token_count, width = tokens.shape
    rows_in = wq.shape[0]
    q_width = wq.shape[1]
    kv_width = wk.shape[1]
    q_heads = q_width // HD
    kv_heads = kv_width // HD
    block = wo.shape[1]
    segments = token_count // SEG
    hops = n // 2
    per_head = n // heads_axis
    wo_parts = 2 if block % (2 * HD) == 0 else 1
    kinds = 4
    gain = norm_gain.reshape(n, 1, rows_in)
    anywhere = pl.BlockSpec(memory_space=pl.ANY)
    near = pl.BlockSpec(memory_space=pltpu.VMEM)
    scalars = pl.BlockSpec(memory_space=pltpu.SMEM)
    bf16, f32 = jnp.bfloat16, jnp.float32
    flops = 2 * token_count * (width * (q_width + 2 * kv_width) + q_width * width)
    return pl.pallas_call(
        functools.partial(layer_kernel, n, heads_axis, wo_parts),
        out_shape=jax.ShapeDtypeStruct((token_count, per_head * block), bf16),
        in_specs=[anywhere, near, anywhere, anywhere, anywhere, anywhere, scalars, near, near],
        out_specs=near,
        scratch_shapes=[
            pltpu.VMEM((n, token_count, rows_in), bf16),
            pltpu.VMEM((n, rows_in, 2 * kv_width), bf16),
            pltpu.VMEM((n, 2, rows_in, q_width // 2), bf16),
            pltpu.VMEM((n, wo_parts, q_width, block // wo_parts), bf16),
            pltpu.VMEM((n, kv_heads * MEM_ROWS, HD), bf16),
            pltpu.VMEM((token_count, 2 * kv_width), f32),
            pltpu.VMEM((token_count, q_width), f32),
            pltpu.VMEM((kv_heads, token_count, HD), bf16),
            pltpu.VMEM((kv_heads, token_count, HD), bf16),
            pltpu.VMEM((q_heads, token_count, HD), bf16),
            pltpu.VMEM((segments, kv_heads, HD, HD), f32),
            pltpu.VMEM((segments, kv_heads, 8, HD), f32),
            pltpu.VMEM((segments, kv_heads, HD, 2 * HD), bf16),
            pltpu.VMEM((token_count, q_width), bf16),
            pltpu.VMEM((wo_parts, n // 2, token_count, block // wo_parts), bf16),
            pltpu.VMEM((wo_parts, per_head, token_count, block // wo_parts), bf16),
            pltpu.SemaphoreType.DMA((kinds, 2, hops, 2)),
            pltpu.SemaphoreType.DMA((kinds, 2, hops, 2)),
            pltpu.SemaphoreType.DMA((wo_parts, n // 2)),
            pltpu.SemaphoreType.DMA((wo_parts, n // 2)),
            pltpu.SemaphoreType.DMA((wo_parts, per_head)),
            pltpu.SemaphoreType.DMA((wo_parts, per_head)),
            pltpu.SemaphoreType.DMA((4 + wo_parts + n,)),
        ],
        compiler_params=pltpu.CompilerParams(
            collective_id=0, has_side_effects=True, vmem_limit_bytes=60 * 1024 * 1024
        ),
        cost_estimate=pl.CostEstimate(
            flops=flops, bytes_accessed=2 * token_count * width, transcendentals=0
        ),
    )(tokens, gain, wq, wk, wv, wo, gate_bias, mem_init, norm_init.reshape(kv_heads, 1, HD))


def solution(mesh):
    placed = (
        P("seq", None),
        P(),
        P("seq", "head"),
        P("seq", "head"),
        P("seq", "head"),
        P("head", "seq"),
        P("head"),
        P("head", None, None),
        P("head", None),
    )
    return jax.shard_map(
        functools.partial(per_device, mesh.shape["seq"], mesh.shape["head"]),
        mesh=mesh,
        in_specs=placed,
        out_specs=P("seq", "head"),
        check_vma=False,
    )
```

```python
import functools
import math

import jax
import jax.numpy as jnp
from jax import lax
from jax.experimental import pallas as pl
from jax.experimental.pallas import tpu as pltpu
from jax.sharding import PartitionSpec as P

HD = 128
SEG = 512
NORM_ROWS = 16
MEM_ROWS = HD + NORM_ROWS
MESH = pl.DeviceIdType.MESH
LOG2E = math.log2(math.e)


def feature_map(values_in):
    return jnp.where(values_in > 0, values_in + 1.0, jnp.exp(jnp.minimum(values_in, 0.0)))


def layer_kernel(
    n,
    heads_axis,
    wo_parts,
    tokens,
    gain,
    wq,
    wk,
    wv,
    wo,
    gates,
    mem_init,
    norm_init,
    out,
    normed,
    kv_full,
    q_full,
    wo_full,
    mem_full,
    acc_kv,
    acc_q,
    keys,
    vals,
    queries,
    deltas,
    delta_norms,
    memory,
    mixed,
    got,
    far,
    xgot,
    ring_send,
    ring_recv,
    give_send,
    give_recv,
    far_send,
    far_recv,
    x_send,
    x_recv,
    load_sem,
):
    me = lax.axis_index("seq")
    head = lax.axis_index("head")
    hops = n // 2
    per_head = n // heads_axis
    rows_in = wq.shape[0]
    token_count = tokens.shape[0]
    kv_width = wk.shape[1]
    q_width = wq.shape[1]
    q_part = q_width // 2
    q_heads = q_width // HD
    kv_heads = kv_width // HD
    group = q_heads // kv_heads
    segments = token_count // SEG
    width = tokens.shape[1]
    block = wo.shape[1]
    sub = block // wo_parts
    tile = 256
    kv_kind, q_kind, wo_kind, mem_kind = range(4)

    odd = lax.rem(me, 2)
    pos = (1 - odd) * lax.div(me, 2) + odd * (n - 1 - lax.div(me, 2))

    def seq_of(place):
        place = lax.rem(place + n, n)
        far = lax.div(place, hops)
        return (1 - far) * 2 * place + far * (2 * (n - place) - 1)

    sides = (seq_of(pos + 1), seq_of(pos - 1))
    core = lax.rem(head, 2)
    partner = head + 1 - 2 * core
    chip = lax.div(head, 2)
    others = [lax.rem(head + 2 + i - core, heads_axis) for i in range(2)]

    loads = [
        pltpu.make_async_copy(wk, kv_full.at[me, :, pl.ds(0, kv_width)], load_sem.at[0]),
        pltpu.make_async_copy(wv, kv_full.at[me, :, pl.ds(kv_width, kv_width)], load_sem.at[1]),
    ]
    for part in range(2):
        loads.append(
            pltpu.make_async_copy(
                wq.at[:, pl.ds(part * q_part, q_part)], q_full.at[me, part], load_sem.at[2 + part]
            )
        )
    for part in range(wo_parts):
        loads.append(
            pltpu.make_async_copy(
                wo.at[:, pl.ds(part * sub, sub)], wo_full.at[me, part], load_sem.at[4 + part]
            )
        )
    weight_loads = len(loads)
    for i in range(n):
        loads.append(
            pltpu.make_async_copy(
                tokens.at[:, pl.ds(i * rows_in, rows_in)], normed.at[i], load_sem.at[weight_loads + i]
            )
        )
    for load in loads:
        load.start()

    barrier = pltpu.get_barrier_semaphore()
    for side in sides:
        pl.semaphore_signal(barrier, inc=1, device_id=(side, head), device_id_type=MESH)
    for other in (partner, others[0], others[1]):
        pl.semaphore_signal(barrier, inc=1, device_id=(me, other), device_id_type=MESH)
    pl.semaphore_wait(barrier, 5)

    fulls = (kv_full, q_full, wo_full, mem_full)

    def part_of(kind, owner, part):
        if kind == q_kind or (kind == wo_kind and wo_parts == 2):
            return fulls[kind].at[owner, part]
        whole = fulls[kind].at[owner, 0] if kind == wo_kind else fulls[kind].at[owner]
        half = whole.shape[0] // 2
        return whole.at[pl.ds(part * half, half)]

    def ring(kind, way, hop, part):
        owner = seq_of(pos - hop + 1) if way == 0 else seq_of(pos + hop - 1)
        view = part_of(kind, owner, part)
        return pltpu.make_async_remote_copy(
            src_ref=view,
            dst_ref=view,
            send_sem=ring_send.at[kind, way, hop - 1, part],
            recv_sem=ring_recv.at[kind, way, hop - 1, part],
            device_id=(sides[way], head),
            device_id_type=MESH,
        )

    def arrival(kind, way, hop, part):
        owner = seq_of(pos - hop) if way == 0 else seq_of(pos + hop)
        view = part_of(kind, owner, part)
        return pltpu.make_async_remote_copy(
            src_ref=view,
            dst_ref=view,
            send_sem=ring_send.at[kind, way, hop - 1, part],
            recv_sem=ring_recv.at[kind, way, hop - 1, part],
            device_id=(sides[way], head),
            device_id_type=MESH,
        )

    def send_first(kind):
        for part in range(2):
            for way in range(2):
                ring(kind, way, 1, part).start()

    def forward(kind, hop):
        for step in range(2):
            for way in range(2):
                part = step if way == 0 else 1 - step
                arrival(kind, way, hop, part).wait_recv()
                if step == 0:
                    ring(kind, way, hop + 1, part).start()
                else:

                    @pl.when(hop + 1 < hops)
                    def _():
                        ring(kind, way, hop + 1, part).start()

    def take_last(kind):
        for way in range(2):
            arrival(kind, way, hops, way).wait_recv()

    loads[0].wait()
    loads[1].wait()
    send_first(kv_kind)
    loads[2].wait()
    loads[3].wait()
    send_first(q_kind)
    for load in loads[4:]:
        load.wait()

    def norm_rows(i, carry):
        rows = pl.ds(pl.multiple_of(i * 64, 64), 64)
        total = jnp.zeros((64, 1), jnp.float32)
        for b in range(n):
            x = normed[b, rows, :].astype(jnp.float32)
            total = total + jnp.sum(x * x, axis=-1, keepdims=True)
        scale = lax.rsqrt(total * (1.0 / width) + 1e-05)
        for b in range(n):
            x = normed[b, rows, :].astype(jnp.float32)
            normed[b, rows, :] = (x * scale * gain[b]).astype(jnp.bfloat16)
        return carry

    lax.fori_loop(0, token_count // 64, norm_rows, 0)

    def project(acc, kind, owner, first=False):
        def body(i, carry):
            rows = pl.ds(pl.multiple_of(i * tile, tile), tile)
            for part in range(2 if kind == q_kind else 1):
                weights = fulls[kind][owner, part] if kind == q_kind else fulls[kind][owner]
                span = weights.shape[-1]
                columns = slice(part * span, (part + 1) * span)
                product = jnp.dot(
                    normed[owner, rows, :], weights, preferred_element_type=jnp.float32
                )
                if first:
                    acc[rows, columns] = product
                else:
                    acc[rows, columns] += product
            return carry

        lax.fori_loop(0, token_count // tile, body, 0)

    def project_hop(acc, kind, hop):
        def body(side, carry):
            project(acc, kind, seq_of(pos - hop + 2 * hop * side))
            return carry

        lax.fori_loop(0, 2, body, 0)

    project(acc_kv, kv_kind, me, True)

    def kv_step(hop, carry):
        forward(kv_kind, hop)
        project_hop(acc_kv, kv_kind, hop)
        return carry

    lax.fori_loop(1, hops, kv_step, 0)
    take_last(kv_kind)
    forward(q_kind, 1)
    project(acc_kv, kv_kind, seq_of(pos + hops))

    for j in range(kv_heads):
        for s in range(segments):
            rows = slice(s * SEG, (s + 1) * SEG)
            key = acc_kv[rows, j * HD : (j + 1) * HD].astype(jnp.bfloat16)
            value = acc_kv[rows, kv_width + j * HD : kv_width + (j + 1) * HD].astype(jnp.bfloat16)
            keys[j, rows, :] = key
            vals[j, rows, :] = value
            feats = feature_map(key.astype(jnp.float32))
            deltas[s, j] = jnp.dot(
                feats.T.astype(jnp.bfloat16), value, preferred_element_type=jnp.float32
            )
            delta_norms[s, j] = jnp.broadcast_to(jnp.sum(feats, axis=0, keepdims=True), (8, HD))
        own = deltas[0, j]
        own_norm = delta_norms[0, j]
        for s in range(1, segments):
            own = own + deltas[s, j]
            own_norm = own_norm + delta_norms[s, j]
        mem_full[me, j * MEM_ROWS : j * MEM_ROWS + HD, :] = own.astype(jnp.bfloat16)
        mem_full[me, j * MEM_ROWS + HD : (j + 1) * MEM_ROWS, :] = jnp.concatenate(
            [own_norm, own_norm], axis=0
        ).astype(jnp.bfloat16)
    send_first(mem_kind)

    project(acc_q, q_kind, me, True)
    project_hop(acc_q, q_kind, 1)

    def q_step(hop, carry):
        forward(q_kind, hop)
        forward(mem_kind, hop - 1)
        project_hop(acc_q, q_kind, hop)
        return carry

    lax.fori_loop(2, hops, q_step, 0)
    send_first(wo_kind)
    forward(mem_kind, hops - 1)
    take_last(q_kind)
    project(acc_q, q_kind, seq_of(pos + hops))
    for h in range(q_heads):
        queries[h] = acc_q[:, h * HD : (h + 1) * HD].astype(jnp.bfloat16)

    exponent_scale = LOG2E / math.sqrt(HD)
    half_seg = SEG // 2

    def scores_of(left, right):
        return lax.dot_general(
            left, right, (((1,), (1,)), ((), ())), preferred_element_type=jnp.float32
        )

    def attend(h, carry):
        j = lax.div(h, group)
        columns = pl.ds(pl.multiple_of(h * HD, HD), HD)
        at_row = lax.broadcasted_iota(jnp.int32, (half_seg, half_seg), 0)
        at_col = lax.broadcasted_iota(jnp.int32, (half_seg, half_seg), 1)
        allowed = at_row >= at_col
        for s in range(segments):
            for t in range(2):
                start = s * SEG + t * half_seg
                query = queries[h, start : start + half_seg, :]
                near_keys = keys[j, start : start + half_seg, :]
                diagonal = jnp.where(allowed, scores_of(query, near_keys), -1e30)
                peak = jnp.max(diagonal, axis=-1, keepdims=True)
                if t:
                    full = scores_of(query, keys[j, start - half_seg : start, :])
                    peak = jnp.maximum(peak, jnp.max(full, axis=-1, keepdims=True))
                expd = jnp.exp2((diagonal - peak) * exponent_scale)
                total = jnp.sum(expd, axis=-1, keepdims=True)
                summed = jnp.dot(
                    expd.astype(jnp.bfloat16),
                    vals[j, start : start + half_seg, :],
                    preferred_element_type=jnp.float32,
                )
                if t:
                    expd = jnp.exp2((full - peak) * exponent_scale)
                    total = total + jnp.sum(expd, axis=-1, keepdims=True)
                    summed = summed + jnp.dot(
                        expd.astype(jnp.bfloat16),
                        vals[j, start - half_seg : start, :],
                        preferred_element_type=jnp.float32,
                    )
                acc_q[start : start + half_seg, columns] = summed / total
        return carry

    lax.fori_loop(0, q_heads // 2, attend, 0)
    forward(wo_kind, 1)
    lax.fori_loop(q_heads // 2, q_heads, attend, 0)

    take_last(mem_kind)
    for j in range(kv_heads):

        def add_earlier(s, carry):
            mem, norm = carry
            earlier = mem_full[s, j * MEM_ROWS : (j + 1) * MEM_ROWS, :].astype(jnp.float32)
            return mem + earlier[:HD], norm + earlier[HD : HD + 8]

        mem, norm = lax.fori_loop(
            0,
            me,
            add_earlier,
            (mem_init[j], jnp.broadcast_to(norm_init[j], (8, HD))),
        )
        for s in range(segments):
            memory[s, j, :, :HD] = mem.astype(jnp.bfloat16)
            memory[s, j, :, HD:] = jnp.broadcast_to(norm[:1], (HD, HD)).T.astype(jnp.bfloat16)
            if s + 1 < segments:
                mem = mem + deltas[s, j]
                norm = norm + delta_norms[s, j]

    def retrieve(h, carry):
        j = lax.div(h, group)
        columns = pl.ds(pl.multiple_of(h * HD, HD), HD)
        gate = 1.0 / (1.0 + jnp.exp(-jnp.full((1, HD), gates[h], jnp.float32)))
        for s in range(segments):
            rows = slice(s * SEG, (s + 1) * SEG)
            feats = feature_map(queries[h, rows, :].astype(jnp.float32)).astype(jnp.bfloat16)
            both = jnp.dot(feats, memory[s, j], preferred_element_type=jnp.float32)
            retrieved = both[:, :HD] / both[:, HD:]
            mixed[rows, columns] = (
                gate * retrieved + (1.0 - gate) * acc_q[rows, columns]
            ).astype(jnp.bfloat16)
        return carry

    lax.fori_loop(0, q_heads, retrieve, 0)

    def summer_of(part, c):
        return part if wo_parts == 2 else lax.rem(lax.rem(c, per_head), 2)

    def far_slot(c):
        return lax.rem(lax.div(c, per_head), 2) * per_head + lax.rem(c, per_head)

    def give_home(part, c):
        index = lax.rem(c, per_head)
        return pltpu.make_async_remote_copy(
            src_ref=normed.at[c, :, pl.ds(part * sub, sub)],
            dst_ref=got.at[part, index],
            send_sem=give_send.at[part, index],
            recv_sem=give_recv.at[part, index],
            device_id=(me, partner),
            device_id_type=MESH,
        )

    def give_far(part, c):
        slot = far_slot(c)
        return pltpu.make_async_remote_copy(
            src_ref=normed.at[c, :, pl.ds(part * sub, sub)],
            dst_ref=far.at[slot],
            send_sem=far_send.at[slot],
            recv_sem=far_recv.at[slot],
            device_id=(me, partner),
            device_id_type=MESH,
        )

    def cross(part, c):
        index = lax.rem(c, per_head)
        return pltpu.make_async_remote_copy(
            src_ref=normed.at[c, :, pl.ds(part * sub, sub)],
            dst_ref=xgot.at[part, index],
            send_sem=x_send.at[far_slot(c)],
            recv_sem=x_recv.at[part, index],
            device_id=(me, lax.div(c, per_head)),
            device_id_type=MESH,
        )

    def cross_arrival(part, c):
        index = lax.rem(c, per_head)
        return pltpu.make_async_remote_copy(
            src_ref=normed.at[c, :, pl.ds(part * sub, sub)],
            dst_ref=xgot.at[part, index],
            send_sem=x_send.at[far_slot(c)],
            recv_sem=x_recv.at[part, index],
            device_id=(me, others[0]),
            device_id_type=MESH,
        )

    def roles(part, c):
        target = lax.div(c, per_head)
        away = lax.div(target, 2) != chip
        mine = summer_of(part, c) == core
        return target, away, mine

    def emit(part, c):
        columns = slice(part * sub, (part + 1) * sub)

        def body(i, carry):
            rows = pl.ds(pl.multiple_of(i * tile, tile), tile)
            normed[c, rows, columns] = jnp.dot(
                mixed[rows, :], wo_full[c, part], preferred_element_type=jnp.float32
            ).astype(jnp.bfloat16)
            return carry

        lax.fori_loop(0, token_count // tile, body, 0)
        target, away, mine = roles(part, c)

        @pl.when(away & jnp.logical_not(mine))
        def _():
            give_far(part, c).start()

        @pl.when(target == partner)
        def _():
            give_home(part, c).start()

    def finish(part, c):
        target, away, mine = roles(part, c)
        columns = slice(part * sub, (part + 1) * sub)
        slot = far_slot(c)

        @pl.when(away & mine)
        def _():
            give_far(part, c).wait_recv()

            def body(i, carry):
                rows = pl.ds(pl.multiple_of(i * tile, tile), tile)
                normed[c, rows, columns] = (
                    normed[c, rows, columns].astype(jnp.float32)
                    + far[slot, rows, :].astype(jnp.float32)
                ).astype(jnp.bfloat16)
                return carry

            lax.fori_loop(0, token_count // tile, body, 0)
            cross(part, c).start()

    def each_block(work, part, hop):
        def side_step(side, carry):
            work(part, seq_of(pos - hop + 2 * hop * side))
            return carry

        lax.fori_loop(0, 2 - lax.div(1, hop + 1), side_step, 0)

    def emits(hop):
        for part in range(wo_parts):
            each_block(emit, part, hop)

    def finishes(hop):
        for part in range(wo_parts):
            each_block(finish, part, hop)

    def collect(part):
        for o in range(per_head):
            c = head * per_head + o
            give_home(part, c).wait_recv()
            cross_arrival(part, c).wait_recv()
            columns = slice(part * sub, (part + 1) * sub)
            placed = slice(o * block + part * sub, o * block + (part + 1) * sub)

            def body(i, carry):
                rows = pl.ds(pl.multiple_of(i * tile, tile), tile)
                out[rows, placed] = (
                    normed[c, rows, columns].astype(jnp.float32)
                    + got[part, o, rows, :].astype(jnp.float32)
                    + xgot[part, o, rows, :].astype(jnp.float32)
                ).astype(jnp.bfloat16)
                return carry

            lax.fori_loop(0, token_count // tile, body, 0)

    last_owner = seq_of(pos + hops)
    emits(jnp.int32(0))
    forward(wo_kind, 2)
    emits(jnp.int32(1))
    finishes(jnp.int32(0))
    emits(jnp.int32(2))
    finishes(jnp.int32(1))

    def out_step(hop, carry):
        finishes(hop - 1)
        forward(wo_kind, hop)
        emits(hop)
        return carry

    lax.fori_loop(3, hops, out_step, 0)
    if wo_parts == 2:
        finishes(jnp.int32(hops - 1))
        for way in range(2):
            arrival(wo_kind, way, hops, way).wait_recv()
            emit(way, last_owner)
        for way in range(2):
            finish(way, last_owner)
    else:
        take_last(wo_kind)
        emit(0, last_owner)
        finishes(jnp.int32(hops - 1))
        finish(0, last_owner)
    for part in range(wo_parts):
        collect(part)

    for kind in range(len(fulls)):

        def drain(hop, carry):
            for way in range(2):
                for part in range(2):
                    ring(kind, way, hop, part).wait_send()
            return carry

        lax.fori_loop(1, hops, drain, 0)
        for way in range(2):
            ring(kind, way, hops, way).wait_send()

    def drain_out(c, carry):
        for part in range(wo_parts):
            target, away, mine = roles(part, c)

            @pl.when(away & jnp.logical_not(mine))
            def _():
                give_far(part, c).wait_send()

            @pl.when(target == partner)
            def _():
                give_home(part, c).wait_send()

            @pl.when(away & mine)
            def _():
                cross(part, c).wait_send()

        return carry

    lax.fori_loop(0, n, drain_out, 0)


def per_device(n, heads_axis, tokens, norm_gain, wq, wk, wv, wo, gate_bias, mem_init, norm_init):
    token_count, width = tokens.shape
    rows_in = wq.shape[0]
    q_width = wq.shape[1]
    kv_width = wk.shape[1]
    q_heads = q_width // HD
    kv_heads = kv_width // HD
    block = wo.shape[1]
    segments = token_count // SEG
    hops = n // 2
    per_head = n // heads_axis
    wo_parts = 2 if block % (2 * HD) == 0 else 1
    kinds = 4
    gain = norm_gain.reshape(n, 1, rows_in)
    anywhere = pl.BlockSpec(memory_space=pl.ANY)
    near = pl.BlockSpec(memory_space=pltpu.VMEM)
    scalars = pl.BlockSpec(memory_space=pltpu.SMEM)
    bf16, f32 = jnp.bfloat16, jnp.float32
    flops = 2 * token_count * (width * (q_width + 2 * kv_width) + q_width * width)
    return pl.pallas_call(
        functools.partial(layer_kernel, n, heads_axis, wo_parts),
        out_shape=jax.ShapeDtypeStruct((token_count, per_head * block), bf16),
        in_specs=[anywhere, near, anywhere, anywhere, anywhere, anywhere, scalars, near, near],
        out_specs=near,
        scratch_shapes=[
            pltpu.VMEM((n, token_count, rows_in), bf16),
            pltpu.VMEM((n, rows_in, 2 * kv_width), bf16),
            pltpu.VMEM((n, 2, rows_in, q_width // 2), bf16),
            pltpu.VMEM((n, wo_parts, q_width, block // wo_parts), bf16),
            pltpu.VMEM((n, kv_heads * MEM_ROWS, HD), bf16),
            pltpu.VMEM((token_count, 2 * kv_width), f32),
            pltpu.VMEM((token_count, q_width), f32),
            pltpu.VMEM((kv_heads, token_count, HD), bf16),
            pltpu.VMEM((kv_heads, token_count, HD), bf16),
            pltpu.VMEM((q_heads, token_count, HD), bf16),
            pltpu.VMEM((segments, kv_heads, HD, HD), f32),
            pltpu.VMEM((segments, kv_heads, 8, HD), f32),
            pltpu.VMEM((segments, kv_heads, HD, 2 * HD), bf16),
            pltpu.VMEM((token_count, q_width), bf16),
            pltpu.VMEM((wo_parts, per_head, token_count, block // wo_parts), bf16),
            pltpu.VMEM((2 * per_head, token_count, block // wo_parts), bf16),
            pltpu.VMEM((wo_parts, per_head, token_count, block // wo_parts), bf16),
            pltpu.SemaphoreType.DMA((kinds, 2, hops, 2)),
            pltpu.SemaphoreType.DMA((kinds, 2, hops, 2)),
            pltpu.SemaphoreType.DMA((wo_parts, per_head)),
            pltpu.SemaphoreType.DMA((wo_parts, per_head)),
            pltpu.SemaphoreType.DMA((2 * per_head,)),
            pltpu.SemaphoreType.DMA((2 * per_head,)),
            pltpu.SemaphoreType.DMA((2 * per_head,)),
            pltpu.SemaphoreType.DMA((wo_parts, per_head)),
            pltpu.SemaphoreType.DMA((4 + wo_parts + n,)),
        ],
        compiler_params=pltpu.CompilerParams(
            collective_id=0, has_side_effects=True, vmem_limit_bytes=60 * 1024 * 1024
        ),
        cost_estimate=pl.CostEstimate(
            flops=flops, bytes_accessed=2 * token_count * width, transcendentals=0
        ),
    )(tokens, gain, wq, wk, wv, wo, gate_bias, mem_init, norm_init.reshape(kv_heads, 1, HD))


def solution(mesh):
    placed = (
        P("seq", None),
        P(),
        P("seq", "head"),
        P("seq", "head"),
        P("seq", "head"),
        P("head", "seq"),
        P("head"),
        P("head", None, None),
        P("head", None),
    )
    return jax.shard_map(
        functools.partial(per_device, mesh.shape["seq"], mesh.shape["head"]),
        mesh=mesh,
        in_specs=placed,
        out_specs=P("seq", "head"),
        check_vma=False,
    )
```

```python
import functools
import math

import jax
import jax.numpy as jnp
from jax import lax
from jax.experimental import pallas as pl
from jax.experimental.pallas import tpu as pltpu
from jax.sharding import PartitionSpec as P

HD = 128
SEG = 512
NORM_ROWS = 16
MEM_ROWS = HD + NORM_ROWS
MESH = pl.DeviceIdType.MESH
LOG2E = math.log2(math.e)


def feature_map(values_in):
    return jnp.where(values_in > 0, values_in + 1.0, jnp.exp(jnp.minimum(values_in, 0.0)))


def layer_kernel(
    n,
    heads_axis,
    wo_parts,
    tokens,
    gain,
    wq,
    wk,
    wv,
    wo,
    gates,
    mem_init,
    norm_init,
    out,
    normed,
    kv_full,
    q_full,
    wo_full,
    mem_full,
    acc_kv,
    acc_q,
    keys,
    vals,
    queries,
    deltas,
    delta_norms,
    memory,
    mixed,
    got,
    xgot,
    ring_send,
    ring_recv,
    give_send,
    give_recv,
    x_send,
    x_recv,
    load_sem,
):
    me = lax.axis_index("seq")
    head = lax.axis_index("head")
    hops = n // 2
    per_head = n // heads_axis
    rows_in = wq.shape[0]
    token_count = tokens.shape[0]
    kv_width = wk.shape[1]
    q_width = wq.shape[1]
    q_part = q_width // 2
    q_heads = q_width // HD
    kv_heads = kv_width // HD
    group = q_heads // kv_heads
    segments = token_count // SEG
    width = tokens.shape[1]
    block = wo.shape[1]
    sub = block // wo_parts
    tile = 256
    kv_kind, q_kinds = 0, (1, 2)
    wo_kinds = tuple(range(3, 3 + wo_parts))
    mem_kind = 3 + wo_parts

    odd = lax.rem(me, 2)
    pos = (1 - odd) * lax.div(me, 2) + odd * (n - 1 - lax.div(me, 2))

    def seq_of(place):
        place = lax.rem(place + n, n)
        far = lax.div(place, hops)
        return (1 - far) * 2 * place + far * (2 * (n - place) - 1)

    sides = (seq_of(pos + 1), seq_of(pos - 1))
    core = lax.rem(head, 2)
    partner = head + 1 - 2 * core
    across = lax.rem(head + heads_axis // 2, heads_axis)

    loads = [
        pltpu.make_async_copy(wk, kv_full.at[me, :, pl.ds(0, kv_width)], load_sem.at[0]),
        pltpu.make_async_copy(wv, kv_full.at[me, :, pl.ds(kv_width, kv_width)], load_sem.at[1]),
    ]
    for part in range(2):
        loads.append(
            pltpu.make_async_copy(
                wq.at[:, pl.ds(part * q_part, q_part)], q_full.at[part, me], load_sem.at[2 + part]
            )
        )
    for part in range(wo_parts):
        loads.append(
            pltpu.make_async_copy(
                wo.at[:, pl.ds(part * sub, sub)], wo_full.at[part, me], load_sem.at[4 + part]
            )
        )
    weight_loads = len(loads)
    for i in range(n):
        loads.append(
            pltpu.make_async_copy(
                tokens.at[:, pl.ds(i * rows_in, rows_in)], normed.at[i], load_sem.at[weight_loads + i]
            )
        )
    for load in loads:
        load.start()

    barrier = pltpu.get_barrier_semaphore()
    for side in sides:
        pl.semaphore_signal(barrier, inc=1, device_id=(side, head), device_id_type=MESH)
    for other in (partner, across):
        pl.semaphore_signal(barrier, inc=1, device_id=(me, other), device_id_type=MESH)
    pl.semaphore_wait(barrier, 4)

    fulls = [kv_full, q_full.at[0], q_full.at[1]]
    fulls += [wo_full.at[part] for part in range(wo_parts)]
    fulls.append(mem_full)

    def ring(kind, way, hop, part):
        owner = seq_of(pos - hop + 1) if way == 0 else seq_of(pos + hop - 1)
        half = fulls[kind].shape[1] // 2
        view = fulls[kind].at[owner, pl.ds(part * half, half)]
        return pltpu.make_async_remote_copy(
            src_ref=view,
            dst_ref=view,
            send_sem=ring_send.at[kind, way, hop - 1, part],
            recv_sem=ring_recv.at[kind, way, hop - 1, part],
            device_id=(sides[way], head),
            device_id_type=MESH,
        )

    def arrival(kind, way, hop, part):
        owner = seq_of(pos - hop) if way == 0 else seq_of(pos + hop)
        half = fulls[kind].shape[1] // 2
        view = fulls[kind].at[owner, pl.ds(part * half, half)]
        return pltpu.make_async_remote_copy(
            src_ref=view,
            dst_ref=view,
            send_sem=ring_send.at[kind, way, hop - 1, part],
            recv_sem=ring_recv.at[kind, way, hop - 1, part],
            device_id=(sides[way], head),
            device_id_type=MESH,
        )

    def send_first(kind):
        for part in range(2):
            for way in range(2):
                ring(kind, way, 1, part).start()

    def forward(kind, hop):
        for step in range(2):
            for way in range(2):
                part = step if way == 0 else 1 - step
                arrival(kind, way, hop, part).wait_recv()
                if step == 0:
                    ring(kind, way, hop + 1, part).start()
                else:

                    @pl.when(hop + 1 < hops)
                    def _():
                        ring(kind, way, hop + 1, part).start()

    def take_last(kind):
        for way in range(2):
            arrival(kind, way, hops, way).wait_recv()

    loads[0].wait()
    loads[1].wait()
    send_first(kv_kind)
    loads[2].wait()
    send_first(q_kinds[0])
    for load in loads[3:]:
        load.wait()

    def norm_rows(i, carry):
        rows = pl.ds(pl.multiple_of(i * 64, 64), 64)
        total = jnp.zeros((64, 1), jnp.float32)
        for b in range(n):
            x = normed[b, rows, :].astype(jnp.float32)
            total = total + jnp.sum(x * x, axis=-1, keepdims=True)
        scale = lax.rsqrt(total * (1.0 / width) + 1e-05)
        for b in range(n):
            x = normed[b, rows, :].astype(jnp.float32)
            normed[b, rows, :] = (x * scale * gain[b]).astype(jnp.bfloat16)
        return carry

    lax.fori_loop(0, token_count // 64, norm_rows, 0)

    def project(acc, columns, kind, owner, first=False):
        def body(i, carry):
            rows = pl.ds(pl.multiple_of(i * tile, tile), tile)
            product = jnp.dot(
                normed[owner, rows, :], fulls[kind][owner], preferred_element_type=jnp.float32
            )
            if first:
                acc[rows, columns] = product
            else:
                acc[rows, columns] += product
            return carry

        lax.fori_loop(0, token_count // tile, body, 0)

    def project_hop(acc, columns, kind, hop):
        def body(side, carry):
            project(acc, columns, kind, seq_of(pos - hop + 2 * hop * side))
            return carry

        lax.fori_loop(0, 2, body, 0)

    kv_columns = slice(0, 2 * kv_width)
    q_columns = [slice(part * q_part, (part + 1) * q_part) for part in range(2)]

    def middle(acc, columns, kind):
        def step(hop, carry):
            forward(kind, hop)
            project_hop(acc, columns, kind, hop - 1)
            return carry

        lax.fori_loop(3, hops, step, 0)

    project(acc_kv, kv_columns, kv_kind, me, True)
    forward(kv_kind, 1)
    project_hop(acc_kv, kv_columns, kv_kind, 1)
    forward(kv_kind, 2)
    middle(acc_kv, kv_columns, kv_kind)
    forward(q_kinds[0], 1)
    project_hop(acc_kv, kv_columns, kv_kind, hops - 1)
    take_last(kv_kind)
    project(acc_kv, kv_columns, kv_kind, seq_of(pos + hops))

    project(acc_q, q_columns[0], q_kinds[0], me, True)
    forward(q_kinds[0], 2)
    send_first(q_kinds[1])
    project_hop(acc_q, q_columns[0], q_kinds[0], 1)

    for j in range(kv_heads):
        for s in range(segments):
            rows = slice(s * SEG, (s + 1) * SEG)
            key = acc_kv[rows, j * HD : (j + 1) * HD].astype(jnp.bfloat16)
            value = acc_kv[rows, kv_width + j * HD : kv_width + (j + 1) * HD].astype(jnp.bfloat16)
            keys[j, rows, :] = key
            vals[j, rows, :] = value
            feats = feature_map(key.astype(jnp.float32))
            deltas[s, j] = jnp.dot(
                feats.T.astype(jnp.bfloat16), value, preferred_element_type=jnp.float32
            )
            delta_norms[s, j] = jnp.broadcast_to(jnp.sum(feats, axis=0, keepdims=True), (8, HD))
        own = deltas[0, j]
        own_norm = delta_norms[0, j]
        for s in range(1, segments):
            own = own + deltas[s, j]
            own_norm = own_norm + delta_norms[s, j]
        mem_full[me, j * MEM_ROWS : j * MEM_ROWS + HD, :] = own.astype(jnp.bfloat16)
        mem_full[me, j * MEM_ROWS + HD : (j + 1) * MEM_ROWS, :] = jnp.concatenate(
            [own_norm, own_norm], axis=0
        ).astype(jnp.bfloat16)
    send_first(mem_kind)

    middle(acc_q, q_columns[0], q_kinds[0])
    forward(q_kinds[1], 1)
    project_hop(acc_q, q_columns[0], q_kinds[0], hops - 1)
    take_last(q_kinds[0])
    project(acc_q, q_columns[0], q_kinds[0], seq_of(pos + hops))

    def round_queries(part):
        for h in range(part * (q_heads // 2), (part + 1) * (q_heads // 2)):
            queries[h] = acc_q[:, h * HD : (h + 1) * HD].astype(jnp.bfloat16)

    exponent_scale = LOG2E / math.sqrt(HD)
    half_seg = SEG // 2

    def scores_of(left, right):
        return lax.dot_general(
            left, right, (((1,), (1,)), ((), ())), preferred_element_type=jnp.float32
        )

    def attend(h, carry):
        j = lax.div(h, group)
        columns = pl.ds(pl.multiple_of(h * HD, HD), HD)
        at_row = lax.broadcasted_iota(jnp.int32, (half_seg, half_seg), 0)
        at_col = lax.broadcasted_iota(jnp.int32, (half_seg, half_seg), 1)
        allowed = at_row >= at_col
        for s in range(segments):
            for t in range(2):
                start = s * SEG + t * half_seg
                query = queries[h, start : start + half_seg, :]
                near_keys = keys[j, start : start + half_seg, :]
                diagonal = jnp.where(allowed, scores_of(query, near_keys), -1e30)
                peak = jnp.max(diagonal, axis=-1, keepdims=True)
                if t:
                    full = scores_of(query, keys[j, start - half_seg : start, :])
                    peak = jnp.maximum(peak, jnp.max(full, axis=-1, keepdims=True))
                expd = jnp.exp2((diagonal - peak) * exponent_scale)
                total = jnp.sum(expd, axis=-1, keepdims=True)
                summed = jnp.dot(
                    expd.astype(jnp.bfloat16),
                    vals[j, start : start + half_seg, :],
                    preferred_element_type=jnp.float32,
                )
                if t:
                    expd = jnp.exp2((full - peak) * exponent_scale)
                    total = total + jnp.sum(expd, axis=-1, keepdims=True)
                    summed = summed + jnp.dot(
                        expd.astype(jnp.bfloat16),
                        vals[j, start - half_seg : start, :],
                        preferred_element_type=jnp.float32,
                    )
                acc_q[start : start + half_seg, columns] = summed / total
        return carry

    half_heads = q_heads // 2
    round_queries(0)
    forward(q_kinds[1], 2)
    send_first(wo_kinds[0])
    forward(mem_kind, 1)
    project(acc_q, q_columns[1], q_kinds[1], me, True)
    project_hop(acc_q, q_columns[1], q_kinds[1], 1)
    lax.fori_loop(0, half_heads // 2, attend, 0)

    def q_step(hop, carry):
        forward(q_kinds[1], hop)
        forward(mem_kind, hop - 1)
        project_hop(acc_q, q_columns[1], q_kinds[1], hop - 1)
        return carry

    lax.fori_loop(3, hops, q_step, 0)
    lax.fori_loop(half_heads // 2, half_heads, attend, 0)
    forward(wo_kinds[0], 1)
    forward(mem_kind, hops - 1)
    project_hop(acc_q, q_columns[1], q_kinds[1], hops - 1)
    take_last(q_kinds[1])
    project(acc_q, q_columns[1], q_kinds[1], seq_of(pos + hops))
    round_queries(1)
    forward(wo_kinds[0], 2)
    if wo_parts > 1:
        send_first(wo_kinds[1])
    lax.fori_loop(half_heads, q_heads, attend, 0)

    def pass_on(kind):
        def step(hop, carry):
            forward(kind, hop)
            return carry

        lax.fori_loop(3, hops, step, 0)

    pass_on(wo_kinds[0])

    take_last(mem_kind)
    for j in range(kv_heads):

        def add_earlier(s, carry):
            mem, norm = carry
            earlier = mem_full[s, j * MEM_ROWS : (j + 1) * MEM_ROWS, :].astype(jnp.float32)
            return mem + earlier[:HD], norm + earlier[HD : HD + 8]

        mem, norm = lax.fori_loop(
            0,
            me,
            add_earlier,
            (mem_init[j], jnp.broadcast_to(norm_init[j], (8, HD))),
        )
        for s in range(segments):
            memory[s, j, :, :HD] = mem.astype(jnp.bfloat16)
            memory[s, j, :, HD:] = jnp.broadcast_to(norm[:1], (HD, HD)).T.astype(jnp.bfloat16)
            if s + 1 < segments:
                mem = mem + deltas[s, j]
                norm = norm + delta_norms[s, j]

    def retrieve(h, carry):
        j = lax.div(h, group)
        columns = pl.ds(pl.multiple_of(h * HD, HD), HD)
        gate = 1.0 / (1.0 + jnp.exp(-jnp.full((1, HD), gates[h], jnp.float32)))
        for s in range(segments):
            rows = slice(s * SEG, (s + 1) * SEG)
            feats = feature_map(queries[h, rows, :].astype(jnp.float32)).astype(jnp.bfloat16)
            both = jnp.dot(feats, memory[s, j], preferred_element_type=jnp.float32)
            retrieved = both[:, :HD] / both[:, HD:]
            mixed[rows, columns] = (
                gate * retrieved + (1.0 - gate) * acc_q[rows, columns]
            ).astype(jnp.bfloat16)
        return carry

    lax.fori_loop(0, q_heads, retrieve, 0)

    def place_of(c):
        target = lax.div(c, per_head)
        slot = lax.div(target, 2) * per_head + lax.rem(c, per_head)
        return target, slot

    def give(part, c):
        target, slot = place_of(c)
        return pltpu.make_async_remote_copy(
            src_ref=normed.at[c, :, pl.ds(part * sub, sub)],
            dst_ref=got.at[part, slot],
            send_sem=give_send.at[part, slot],
            recv_sem=give_recv.at[part, slot],
            device_id=(me, partner),
            device_id_type=MESH,
        )

    def cross(part, c):
        index = lax.rem(c, per_head)
        return pltpu.make_async_remote_copy(
            src_ref=normed.at[c, :, pl.ds(part * sub, sub)],
            dst_ref=xgot.at[part, index],
            send_sem=x_send.at[part, index],
            recv_sem=x_recv.at[part, index],
            device_id=(me, across),
            device_id_type=MESH,
        )

    def emit(part, c):
        columns = slice(part * sub, (part + 1) * sub)

        def body(i, carry):
            rows = pl.ds(pl.multiple_of(i * tile, tile), tile)
            normed[c, rows, columns] = jnp.dot(
                mixed[rows, :], wo_full[part, c], preferred_element_type=jnp.float32
            ).astype(jnp.bfloat16)
            return carry

        lax.fori_loop(0, token_count // tile, body, 0)
        target, slot = place_of(c)

        @pl.when(lax.rem(target, 2) != core)
        def _():
            give(part, c).start()

    def finish(part, c):
        target, slot = place_of(c)
        columns = slice(part * sub, (part + 1) * sub)

        @pl.when(lax.rem(target, 2) == core)
        def _():
            give(part, c).wait_recv()

            def body(i, carry):
                rows = pl.ds(pl.multiple_of(i * tile, tile), tile)
                normed[c, rows, columns] = (
                    normed[c, rows, columns].astype(jnp.float32)
                    + got[part, slot, rows, :].astype(jnp.float32)
                ).astype(jnp.bfloat16)
                return carry

            @pl.when(target != head)
            def _():
                lax.fori_loop(0, token_count // tile, body, 0)
                cross(part, c).start()

    def out_hops(part, first, last):
        def out_step(hop, carry):
            def emit_side(side, inner):
                emit(part, seq_of(pos - hop + 2 * hop * side))
                return inner

            def finish_side(side, inner):
                finish(part, seq_of(pos - hop + 2 * hop * side))
                return inner

            lax.fori_loop(0, 2, emit_side, 0)
            lax.fori_loop(0, 2, finish_side, 0)
            return carry

        lax.fori_loop(first, last + 1, out_step, 0)

    def out_one(part, c):
        emit(part, c)
        finish(part, c)

    def collect(part):
        for o in range(per_head):
            c = head * per_head + o
            cross(part, c).wait_recv()
            slot = lax.div(head, 2) * per_head + o
            columns = slice(part * sub, (part + 1) * sub)
            placed = slice(o * block + part * sub, o * block + (part + 1) * sub)

            def body(i, carry):
                rows = pl.ds(pl.multiple_of(i * tile, tile), tile)
                out[rows, placed] = (
                    normed[c, rows, columns].astype(jnp.float32)
                    + got[part, slot, rows, :].astype(jnp.float32)
                    + xgot[part, o, rows, :].astype(jnp.float32)
                ).astype(jnp.bfloat16)
                return carry

            lax.fori_loop(0, token_count // tile, body, 0)

    for part in range(wo_parts):
        kind = wo_kinds[part]
        more = part + 1 < wo_parts
        if more:
            forward(wo_kinds[part + 1], 1)
        out_one(part, me)
        out_hops(part, 1, hops - 2)
        if more:
            forward(wo_kinds[part + 1], 2)
        out_hops(part, hops - 1, hops - 1)
        if part:
            collect(part - 1)
        take_last(kind)
        out_one(part, seq_of(pos + hops))
        if more:
            pass_on(wo_kinds[part + 1])
    collect(wo_parts - 1)

    for kind in range(len(fulls)):

        def drain(hop, carry):
            for way in range(2):
                for part in range(2):
                    ring(kind, way, hop, part).wait_send()
            return carry

        lax.fori_loop(1, hops, drain, 0)
        for way in range(2):
            ring(kind, way, hops, way).wait_send()

    def drain_out(c, carry):
        target, slot = place_of(c)
        for part in range(wo_parts):

            @pl.when(lax.rem(target, 2) != core)
            def _():
                give(part, c).wait_send()

            @pl.when((lax.rem(target, 2) == core) & (target != head))
            def _():
                cross(part, c).wait_send()

        return carry

    lax.fori_loop(0, n, drain_out, 0)


def per_device(n, heads_axis, tokens, norm_gain, wq, wk, wv, wo, gate_bias, mem_init, norm_init):
    token_count, width = tokens.shape
    rows_in = wq.shape[0]
    q_width = wq.shape[1]
    kv_width = wk.shape[1]
    q_heads = q_width // HD
    kv_heads = kv_width // HD
    block = wo.shape[1]
    segments = token_count // SEG
    hops = n // 2
    per_head = n // heads_axis
    wo_parts = 2 if block % (2 * HD) == 0 else 1
    kinds = 4 + wo_parts
    gain = norm_gain.reshape(n, 1, rows_in)
    anywhere = pl.BlockSpec(memory_space=pl.ANY)
    near = pl.BlockSpec(memory_space=pltpu.VMEM)
    scalars = pl.BlockSpec(memory_space=pltpu.SMEM)
    bf16, f32 = jnp.bfloat16, jnp.float32
    flops = 2 * token_count * (width * (q_width + 2 * kv_width) + q_width * width)
    return pl.pallas_call(
        functools.partial(layer_kernel, n, heads_axis, wo_parts),
        out_shape=jax.ShapeDtypeStruct((token_count, per_head * block), bf16),
        in_specs=[anywhere, near, anywhere, anywhere, anywhere, anywhere, scalars, near, near],
        out_specs=near,
        scratch_shapes=[
            pltpu.VMEM((n, token_count, rows_in), bf16),
            pltpu.VMEM((n, rows_in, 2 * kv_width), bf16),
            pltpu.VMEM((2, n, rows_in, q_width // 2), bf16),
            pltpu.VMEM((wo_parts, n, q_width, block // wo_parts), bf16),
            pltpu.VMEM((n, kv_heads * MEM_ROWS, HD), bf16),
            pltpu.VMEM((token_count, 2 * kv_width), f32),
            pltpu.VMEM((token_count, q_width), f32),
            pltpu.VMEM((kv_heads, token_count, HD), bf16),
            pltpu.VMEM((kv_heads, token_count, HD), bf16),
            pltpu.VMEM((q_heads, token_count, HD), bf16),
            pltpu.VMEM((segments, kv_heads, HD, HD), f32),
            pltpu.VMEM((segments, kv_heads, 8, HD), f32),
            pltpu.VMEM((segments, kv_heads, HD, 2 * HD), bf16),
            pltpu.VMEM((token_count, q_width), bf16),
            pltpu.VMEM((wo_parts, n // 2, token_count, block // wo_parts), bf16),
            pltpu.VMEM((wo_parts, per_head, token_count, block // wo_parts), bf16),
            pltpu.SemaphoreType.DMA((kinds, 2, hops, 2)),
            pltpu.SemaphoreType.DMA((kinds, 2, hops, 2)),
            pltpu.SemaphoreType.DMA((wo_parts, n // 2)),
            pltpu.SemaphoreType.DMA((wo_parts, n // 2)),
            pltpu.SemaphoreType.DMA((wo_parts, per_head)),
            pltpu.SemaphoreType.DMA((wo_parts, per_head)),
            pltpu.SemaphoreType.DMA((4 + wo_parts + n,)),
        ],
        compiler_params=pltpu.CompilerParams(
            collective_id=0, has_side_effects=True, vmem_limit_bytes=60 * 1024 * 1024
        ),
        cost_estimate=pl.CostEstimate(
            flops=flops, bytes_accessed=2 * token_count * width, transcendentals=0
        ),
    )(tokens, gain, wq, wk, wv, wo, gate_bias, mem_init, norm_init.reshape(kv_heads, 1, HD))


def solution(mesh):
    placed = (
        P("seq", None),
        P(),
        P("seq", "head"),
        P("seq", "head"),
        P("seq", "head"),
        P("head", "seq"),
        P("head"),
        P("head", None, None),
        P("head", None),
    )
    return jax.shard_map(
        functools.partial(per_device, mesh.shape["seq"], mesh.shape["head"]),
        mesh=mesh,
        in_specs=placed,
        out_specs=P("seq", "head"),
        check_vma=False,
    )
```
